32 devices in a mesh: grp: 2 (over x), ang: 16 (over z, y, core).
Axes of the slice: x: 2, y: 2, z: 4, core: 2. Of those that a mesh axis runs over, the one named last changes fastest.
Arguments:
- children: bfloat16 [2, 32, 8, 2, 1, 2048], P(None, ('grp', 'ang')), may hold values from -6 to 6
- present: int32 [32, 8], P(('grp', 'ang')), may hold values 0 or 1
- interp: float32 [8, 8192], replicated, may hold values from -2 to 2
- phase: float32 [8, 8192], replicated, may hold values from -3.140625 to 3.140625
- trans: float32 [2, 316, 8192], P(None, None, 'ang'), may hold values from -0.6 to 0.6
- sources: int32 [32, 8], P('grp'), may hold values from 0 to 31
- trans_ids: int32 [32, 8], P('grp'), may hold values from 0 to 315
- list_len: int32 [32], P('grp'), may hold values from 1 to 8
Outputs:
- received: float32 [2, 32, 2, 1, 8192], P(None, 'grp', None, None, 'ang')
The draws below stay inside these ranges and needn't reach their ends.
All inputs are finite; a program needn't handle non-finite values. No bound on the sum of `present` on one device may be relied on, other than what follows from the above.
Results may differ from the reference program's by a relative error of at most 0.0029.
Values may be sent and summed in bfloat16 or wider, within the bound.
A program may use at most 128 MiB of HBM per device.

```python
import jax
import jax.numpy as jnp
from jax import lax

HW = 4
POL = 2
CH = 8
R = 1
LIST = 8
NT = 316
TAPS = 8
K = 8192
KC = 2048
CLUSTERS = 32


def touch_ends(values, stream_key, low, largest):
    spot = [jax.random.randint(jax.random.fold_in(stream_key, axis), (), 0, length) for axis, length in enumerate(values.shape)]
    main_axis = values.shape.index(max(values.shape))
    next_to = spot[:main_axis] + [(spot[main_axis] + 1) % values.shape[main_axis]] + spot[main_axis + 1:]
    return values.at[tuple(spot)].set(low).at[tuple(next_to)].set(largest)


def levels(stream_key, dims, shards, smallest, high):
    gain, own = 1.0, jax.random.fold_in(stream_key, 6)
    for dim, parts in shards:
        draws = jnp.exp(jax.random.uniform(jax.random.fold_in(own, dim), (parts,), jnp.float32, smallest / len(shards), high / len(shards)))
        gain = gain * jnp.repeat(draws, dims[dim] // parts).reshape([-1 if axis == dim else 1 for axis in range(len(dims))])
    return gain


def normal_values(rng, shape, scale, most, shards=(), held_as=jnp.bfloat16):
    array = scale * jax.random.normal(rng, shape, jnp.float32)
    if shards:
        array = array * levels(rng, shape, shards, -0.22, 0.18)
    return jnp.clip(array, -most, most).astype(held_as)


def setup_inputs(seed: int = 0) -> dict:
    key_list = jax.random.split(jax.random.key(seed), 9)
    return {
        "children": normal_values(key_list[0], (2, CLUSTERS, CH, POL, R, KC), 1.0, 6.0, ((1, 32),)),
        "present": touch_ends((jax.random.randint(key_list[1], (CLUSTERS, CH), 0, 4) < 3).astype(jnp.int32), jax.random.fold_in(key_list[1], 1), 0, 1),
        "interp": normal_values(key_list[2], (TAPS, K), TAPS ** -0.5, 2.0, (), jnp.float32),
        "phase": jnp.clip(jax.random.uniform(key_list[3], (CH, K), jnp.float32, -3.140625, 3.140625), -3.140625, 3.140625),
        "trans": normal_values(key_list[4], (2, NT, K), 0.1, 0.6, ((2, 16),), jnp.float32),
        "sources": touch_ends(jax.random.randint(key_list[5], (CLUSTERS, LIST), 0, CLUSTERS), jax.random.fold_in(key_list[5], 1), 0, CLUSTERS - 1).astype(jnp.int32),
        "trans_ids": touch_ends(jax.random.randint(key_list[6], (CLUSTERS, LIST), 0, NT), jax.random.fold_in(key_list[6], 1), 0, NT - 1).astype(jnp.int32),
        "list_len": touch_ends(jax.random.randint(key_list[7], (CLUSTERS,), 1, LIST + 1), jax.random.fold_in(key_list[7], 1), 1, LIST).astype(jnp.int32),
    }


def aggregate(extended, weights, cosine, sine_part, coarse_len):
    taps_count = weights.shape[0]
    octants = extended.shape[2]
    fine_len = 4 * coarse_len
    real_acc = None
    imag_acc = None
    for octant in range(octants):
        spread = jnp.repeat(extended[:, :, octant].astype(jnp.float32), 4, axis=-1)
        refined = jnp.zeros(spread.shape[:-1] + (fine_len,), jnp.float32)
        for stencil in range(taps_count):
            window = spread[..., 4 * stencil:4 * stencil + fine_len]
            refined = refined + window * weights[stencil]
        cos_row = cosine[octant]
        sin_row = sine_part[octant]
        real_term = refined[0] * cos_row - refined[1] * sin_row
        imag_term = refined[0] * sin_row + refined[1] * cos_row
        if real_acc is None:
            real_acc = jnp.zeros_like(real_term) + real_term
            imag_acc = jnp.zeros_like(imag_term) + imag_term
        else:
            real_acc = real_acc + real_term
            imag_acc = imag_acc + imag_term
    return jnp.stack([real_acc, imag_acc]).astype(jnp.bfloat16)


def reference(children, present, interp, phase, trans, sources, trans_ids, list_len):
    cosine = jnp.cos(phase)
    sine_part = jnp.sin(phase)
    coarse_len = children.shape[-1]

    def one_parent(pair):
        kept_children = pair[0] * pair[1].astype(jnp.bfloat16)[None, :, None, None, None]
        extended = jnp.concatenate([kept_children[..., -HW:], kept_children, kept_children[..., :HW]], axis=-1)
        return aggregate(extended[:, None], interp, cosine, sine_part, coarse_len)[:, 0]

    parents = lax.map(one_parent, (jnp.moveaxis(children, 1, 0), present))
    parents = jnp.moveaxis(parents, 0, 1)

    def one_receiver(triple):
        source_ids, operator_ids, used = triple
        real_sum = jnp.zeros(parents.shape[2:], jnp.float32)
        imag_sum = jnp.zeros(parents.shape[2:], jnp.float32)
        for position in range(LIST):
            source_rows = parents[:, source_ids[position]].astype(jnp.float32)
            operator_cols = trans[:, operator_ids[position]][:, None, None, :]
            active = (position < used).astype(jnp.float32)
            real_sum = real_sum + active * (operator_cols[0] * source_rows[0] - operator_cols[1] * source_rows[1])
            imag_sum = imag_sum + active * (operator_cols[0] * source_rows[1] + operator_cols[1] * source_rows[0])
        return jnp.stack([real_sum, imag_sum])

    result = lax.map(one_receiver, (sources, trans_ids, list_len))
    return jnp.moveaxis(result, 0, 1)
```

```python
import functools

import jax
import jax.numpy as jnp
from jax import lax
from jax.experimental import pallas as pl
from jax.experimental.pallas import tpu as pltpu
from jax.sharding import PartitionSpec as P

MESH = pl.DeviceIdType.MESH
F32, BF16 = jnp.float32, jnp.bfloat16
LANES, SUBS = 128, 8

SIN_COEFFS = (1.0, -1.0 / 6, 1.0 / 120, -1.0 / 5040, 1.0 / 362880, -1.0 / 39916800)
COS_COEFFS = (1.0, -1.0 / 2, 1.0 / 24, -1.0 / 720, 1.0 / 40320, -1.0 / 3628800, 1.0 / 479001600)


def horner(coeffs, x):
    total = jnp.full_like(x, coeffs[-1])
    for coeff in coeffs[-2::-1]:
        total = total * x + coeff
    return total


def sin_cos(angle):
    half = angle * 0.5
    square = half * half
    sine = half * horner(SIN_COEFFS, square)
    cosine = horner(COS_COEFFS, square)
    return 2.0 * sine * cosine, 1.0 - 2.0 * sine * sine


def iota(shape, axis):
    return lax.broadcasted_iota(jnp.int32, shape, axis)


def sublane_sums(rows, sub):
    low = (sub & 4) == 0
    rows = [
        jnp.where(low, rows[i], rows[i + 4]) + pltpu.roll(jnp.where(low, rows[i + 4], rows[i]), 4, 0)
        for i in range(4)
    ]
    for step in (2, 1):
        low = (sub & step) == 0
        rows = [
            jnp.where(low, rows[i], rows[i + step])
            + jnp.where(low, pltpu.roll(rows[i], SUBS - step, 0), pltpu.roll(rows[i + step], step, 0))
            for i in range(step)
        ]
    return rows[0]


def kernel(
    grp_size, ang_size, unroll,
    children, present, interp, phase, trans, sources, trans_ids, list_len,
    out,
    child_v, interp_v, phase_v, trans_v, slabs, lhs, send, recv, picked, patterns, turned,
    load_sems, send_sem, recv_sem,
):
    my_grp, my_ang = lax.axis_index("grp"), lax.axis_index("ang")
    devices = grp_size * ang_size
    me = my_grp * ang_size + my_ang

    loads = [
        pltpu.make_async_copy(src, dst, load_sems.at[i])
        for i, (src, dst) in enumerate(
            ((children, child_v), (interp, interp_v), (phase, phase_v), (trans, trans_v))
        )
    ]
    for load in loads:
        load.start()

    barrier = pltpu.get_barrier_semaphore()

    def greet(step, carry):
        other = lax.rem(me + step, devices)
        pl.semaphore_signal(
            barrier, inc=1, device_id=(other // ang_size, lax.rem(other, ang_size)), device_id_type=MESH
        )
        return carry

    lax.fori_loop(1, devices, greet, 0)

    sub = iota((SUBS, LANES), 0)
    octants = present.shape[1]
    mask = jnp.zeros((SUBS, LANES), F32)
    for octant in range(octants):
        mask = jnp.where(sub == octant, present[0, octant].astype(F32), mask)

    loads[0].wait()
    coarse_tiles = slabs.shape[0]
    for tile in range(coarse_tiles):
        part = child_v[:, :, tile * LANES:(tile + 1) * LANES].astype(F32)
        for row in range(part.shape[0]):
            slabs[tile, 2 * row:2 * row + 2, :] = part[row]
    half_width = interp.shape[0] // 2
    lane = iota((SUBS, LANES), 1)

    def shifted(here, before, by):
        return jnp.where(lane < by, pltpu.roll(before, by, 1), pltpu.roll(here, by, 1))

    for pol in range(2):
        groups = []
        for reim in range(2):
            tiles = [
                slabs[tile, pl.ds(2 * octants * reim + pol, octants, stride=2), :] * mask
                for tile in range(coarse_tiles)
            ]
            groups.append(tiles)
        for tile in range(coarse_tiles):
            first = [shifted(g[tile], g[tile - 1], half_width) for g in groups]
            second = [
                shifted(g[(tile + 1) % coarse_tiles], g[tile], half_width + LANES // 2) for g in groups
            ]
            rows = slice(2 * octants * pol, 2 * octants * (pol + 1))
            lhs[tile, 0, rows, :] = jnp.concatenate(first, axis=0).astype(BF16)
            lhs[tile, 1, rows, :] = jnp.concatenate(second, axis=0).astype(BF16)

    loads[1].wait()
    loads[2].wait()

    band_rows = 48
    gap = iota((band_rows, LANES), 0) - iota((band_rows, LANES), 1) // 4
    band = jnp.where((gap >= 0) & (gap < SUBS), 1.0, 0.0).astype(BF16)
    turn = lane // 4

    def banded(weights):
        for step in (1, 2, 4):
            weights = jnp.where((turn & step) != 0, pltpu.roll(weights, step, 0), weights)
        high = weights.astype(BF16)
        low = (weights - high.astype(F32)).astype(BF16)
        return [jnp.concatenate([x] * (band_rows // SUBS), axis=0) * band for x in (high, low)]

    def blank(rows):
        return jnp.zeros((rows, LANES), BF16)

    def one_block(block):
        real, imag = [], []
        for half in range(2):
            x = lhs[block, half]
            cols = []
            for tile in range(2):
                at = pl.multiple_of((4 * block + 2 * half + tile) * LANES, LANES)
                pieces = []
                for piece in banded(interp_v[:, pl.ds(at, LANES)]):
                    pieces += [blank(32 * tile), piece] if tile else [piece]
                    pieces.append(blank(LANES - band_rows - 32 * tile))
                cols.append(jnp.concatenate(pieces, axis=0))
            fine = jnp.dot(
                jnp.concatenate([x, x], axis=1), jnp.concatenate(cols, axis=1), preferred_element_type=F32
            )
            for tile in range(2):
                at = pl.multiple_of((4 * block + 2 * half + tile) * LANES, LANES)
                sine, cosine = sin_cos(phase_v[:, pl.ds(at, LANES)])
                for pol in range(2):
                    re = fine[16 * pol:16 * pol + 8, tile * LANES:(tile + 1) * LANES]
                    im = fine[16 * pol + 8:16 * pol + 16, tile * LANES:(tile + 1) * LANES]
                    real.append(re * cosine - im * sine)
                    imag.append(re * sine + im * cosine)
        return jnp.concatenate([sublane_sums(real, sub), sublane_sums(imag, sub)], axis=0).astype(BF16)

    def post(block):
        for step in range(grp_size):
            grp = lax.rem(my_grp + step, grp_size)

            def away():
                pltpu.make_async_remote_copy(
                    src_ref=send.at[block], dst_ref=recv.at[me], send_sem=send_sem, recv_sem=recv_sem,
                    device_id=(grp, block), device_id_type=MESH,
                ).start()

            if step:
                away()
            else:
                pl.when(block != my_ang)(away)

                @pl.when(block == my_ang)
                def _():
                    pltpu.make_async_copy(send.at[block], recv.at[me], recv_sem).start()

    def blocks_of(step):
        return [lax.rem(my_ang + 1 + step * unroll + i, ang_size) for i in range(unroll)]

    def aggregate(step):
        for block in blocks_of(step):
            send[block] = one_block(block)

    def dispatch(step):
        for block in blocks_of(step):
            post(block)

    aggregate(0)
    pl.semaphore_wait(barrier, devices - 1)
    dispatch(0)

    def advance(step, carry):
        aggregate(step)
        dispatch(step)
        return carry

    lax.fori_loop(1, ang_size // unroll, advance, 0)

    loads[3].wait()
    slots, clusters = sources.shape
    even = (sub & 1) == 0

    def pick(cluster, carry):
        for slot in range(slots):
            both = trans_v[trans_ids[slot, cluster]]
            both = both * jnp.where(slot < list_len[cluster], 1.0, 0.0)
            picked[cluster * slots + slot, 0] = jnp.where(even, both, pltpu.roll(both, 1, 0))
            picked[cluster * slots + slot, 1] = jnp.where(even, pltpu.roll(both, SUBS - 1, 0), both)
        return carry

    lax.fori_loop(0, clusters, pick, 0, unroll=2)

    pltpu.make_async_copy(recv, recv, recv_sem).wait()

    def widen(source, carry):
        patterns[source] = recv[source].astype(F32)
        return carry

    lax.fori_loop(0, devices, widen, 0, unroll=8)

    def receive(cluster, carry):
        real = imag = jnp.zeros((SUBS, LANES), F32)
        for slot in range(slots):
            source = sources[slot, cluster]
            row = cluster * slots + slot
            op_re, op_im = picked[row, 0], picked[row, 1]
            src_re, src_im = patterns[source, 0:SUBS], patterns[source, SUBS:2 * SUBS]
            real += op_re * src_re - op_im * src_im
            imag += op_re * src_im + op_im * src_re
        for part, value in enumerate((real, imag)):
            turned[cluster, part] = value
            for pol in range(2):
                out[part, cluster, 4 * pol:4 * pol + 4, :] = turned[cluster, part, pl.ds(pol, 4, stride=2), :]
        return carry

    lax.fori_loop(0, clusters, receive, 0, unroll=2)

    sent = recv.at[pl.ds(0, devices - 1)]
    pltpu.make_async_copy(sent, sent, send_sem).wait()


def local(grp_size, ang_size, children, present, interp, phase, trans, sources, trans_ids, list_len):
    parts, own, octants, pols, angles, coarse = children.shape
    operators, width = trans.shape[1:]
    clusters, slots = sources.shape
    devices = grp_size * ang_size
    quarters = width // LANES
    assert (parts, own, octants, pols, angles, quarters) == (2, 1, SUBS, 2, 1, 4)
    assert interp.shape[0] == SUBS and interp.shape[1] == ang_size * width == 4 * coarse
    children = children.reshape(parts * octants, pols, coarse)
    trans = trans.transpose(1, 0, 2).reshape(operators, parts, quarters, LANES)
    trans = trans.transpose(0, 2, 1, 3).reshape(operators, quarters * parts, LANES)
    anywhere = pl.BlockSpec(memory_space=pl.ANY)
    scalars = pl.BlockSpec(memory_space=pltpu.SMEM)
    tile_rows = 2 * SUBS
    received = pl.pallas_call(
        functools.partial(kernel, grp_size, ang_size, 4),
        out_shape=jax.ShapeDtypeStruct((parts, clusters, SUBS, LANES), F32),
        in_specs=[anywhere, scalars, anywhere, anywhere, anywhere, scalars, scalars, scalars],
        out_specs=pl.BlockSpec(memory_space=pltpu.VMEM),
        scratch_shapes=[
            pltpu.VMEM(children.shape, BF16),
            pltpu.VMEM(interp.shape, F32),
            pltpu.VMEM(phase.shape, F32),
            pltpu.VMEM(trans.shape, F32),
            pltpu.VMEM((coarse // LANES, parts * octants * pols, LANES), F32),
            pltpu.VMEM((coarse // LANES, 2, parts * octants * pols, LANES), BF16),
            pltpu.VMEM((ang_size, tile_rows, LANES), BF16),
            pltpu.VMEM((devices, tile_rows, LANES), BF16),
            pltpu.VMEM((clusters * slots, 2, SUBS, LANES), F32),
            pltpu.VMEM((devices, tile_rows, LANES), F32),
            pltpu.VMEM((clusters, 2, SUBS, LANES), F32),
            pltpu.SemaphoreType.DMA((4,)),
            pltpu.SemaphoreType.DMA,
            pltpu.SemaphoreType.DMA,
        ],
        compiler_params=pltpu.CompilerParams(
            collective_id=0, has_side_effects=True, vmem_limit_bytes=48 * 1024 * 1024
        ),
    )(children, present, interp, phase, trans, sources.T, trans_ids.T, list_len)
    return received.reshape(parts, clusters, pols, angles, width)


def solution(mesh):
    return jax.shard_map(
        functools.partial(local, mesh.shape["grp"], mesh.shape["ang"]),
        mesh=mesh,
        in_specs=(
            P(None, ("grp", "ang"), None, None, None, None),
            P(("grp", "ang"), None),
            P(),
            P(),
            P(None, None, "ang"),
            P("grp", None),
            P("grp", None),
            P("grp"),
        ),
        out_specs=P(None, "grp", None, None, "ang"),
        check_vma=False,
    )
```

```python
import functools

import jax
import jax.numpy as jnp
from jax import lax
from jax.experimental import pallas as pl
from jax.experimental.pallas import tpu as pltpu
from jax.sharding import PartitionSpec as P

MESH = pl.DeviceIdType.MESH
F32, BF16 = jnp.float32, jnp.bfloat16
LANES, SUBS = 128, 8

SIN_COEFFS = (1.0, -1.0 / 6, 1.0 / 120, -1.0 / 5040, 1.0 / 362880, -1.0 / 39916800)
COS_COEFFS = (1.0, -1.0 / 2, 1.0 / 24, -1.0 / 720, 1.0 / 40320, -1.0 / 3628800, 1.0 / 479001600)


def horner(coeffs, x):
    total = jnp.full_like(x, coeffs[-1])
    for coeff in coeffs[-2::-1]:
        total = total * x + coeff
    return total


def sin_cos(angle):
    half = angle * 0.5
    square = half * half
    sine = half * horner(SIN_COEFFS, square)
    cosine = horner(COS_COEFFS, square)
    return 2.0 * sine * cosine, 1.0 - 2.0 * sine * sine


def iota(shape, axis):
    return lax.broadcasted_iota(jnp.int32, shape, axis)


def sublane_sums(rows, sub):
    low = (sub & 4) == 0
    rows = [
        jnp.where(low, rows[i], rows[i + 4]) + pltpu.roll(jnp.where(low, rows[i + 4], rows[i]), 4, 0)
        for i in range(4)
    ]
    for step in (2, 1):
        low = (sub & step) == 0
        rows = [
            jnp.where(low, rows[i], rows[i + step])
            + jnp.where(low, pltpu.roll(rows[i], SUBS - step, 0), pltpu.roll(rows[i + step], step, 0))
            for i in range(step)
        ]
    return rows[0]


def kernel(
    grp_size, ang_size, unroll,
    children_h, present_h, interp_h, phase_h, trans_h, sources_h, trans_ids_h, list_len_h,
    out,
    child_v, present, interp, phase, trans, sources, trans_ids, list_len, slabs, lhs, send, recv, picked, patterns, turned,
    load_sems, send_sem, recv_sem,
):
    my_grp, my_ang = lax.axis_index("grp"), lax.axis_index("ang")
    devices = grp_size * ang_size
    me = my_grp * ang_size + my_ang

    pairs = (
        (children_h, child_v), (present_h, present), (interp_h, interp), (phase_h, phase),
        (trans_h, trans), (sources_h, sources), (trans_ids_h, trans_ids), (list_len_h, list_len),
    )
    loads = [pltpu.make_async_copy(src, dst, load_sems.at[i]) for i, (src, dst) in enumerate(pairs)]
    for load in loads:
        load.start()

    barrier = pltpu.get_barrier_semaphore()

    def greet(step, carry):
        other = lax.rem(me + step, devices)
        pl.semaphore_signal(
            barrier, inc=1, device_id=(other // ang_size, lax.rem(other, ang_size)), device_id_type=MESH
        )
        return carry

    lax.fori_loop(1, devices, greet, 0)

    loads[0].wait()
    loads[1].wait()
    sub = iota((SUBS, LANES), 0)
    octants = present.shape[1]
    mask = jnp.zeros((SUBS, LANES), F32)
    for octant in range(octants):
        mask = jnp.where(sub == octant, present[0, octant].astype(F32), mask)

    coarse_tiles = slabs.shape[0]
    for tile in range(coarse_tiles):
        part = child_v[:, :, tile * LANES:(tile + 1) * LANES].astype(F32)
        for row in range(part.shape[0]):
            slabs[tile, 2 * row:2 * row + 2, :] = part[row]
    half_width = interp.shape[0] // 2
    lane = iota((SUBS, LANES), 1)

    def shifted(here, before, by):
        return jnp.where(lane < by, pltpu.roll(before, by, 1), pltpu.roll(here, by, 1))

    for pol in range(2):
        groups = []
        for reim in range(2):
            tiles = [
                slabs[tile, pl.ds(2 * octants * reim + pol, octants, stride=2), :] * mask
                for tile in range(coarse_tiles)
            ]
            groups.append(tiles)
        for tile in range(coarse_tiles):
            first = [shifted(g[tile], g[tile - 1], half_width) for g in groups]
            second = [
                shifted(g[(tile + 1) % coarse_tiles], g[tile], half_width + LANES // 2) for g in groups
            ]
            rows = slice(2 * octants * pol, 2 * octants * (pol + 1))
            lhs[tile, 0, rows, :] = jnp.concatenate(first, axis=0).astype(BF16)
            lhs[tile, 1, rows, :] = jnp.concatenate(second, axis=0).astype(BF16)

    loads[2].wait()
    loads[3].wait()

    band_rows = 48
    gap = iota((band_rows, LANES), 0) - iota((band_rows, LANES), 1) // 4
    band = jnp.where((gap >= 0) & (gap < SUBS), 1.0, 0.0).astype(BF16)
    turn = lane // 4

    def banded(weights):
        for step in (1, 2, 4):
            weights = jnp.where((turn & step) != 0, pltpu.roll(weights, step, 0), weights)
        high = weights.astype(BF16)
        low = (weights - high.astype(F32)).astype(BF16)
        return [jnp.concatenate([x] * (band_rows // SUBS), axis=0) * band for x in (high, low)]

    def blank(rows):
        return jnp.zeros((rows, LANES), BF16)

    def one_block(block):
        real, imag = [], []
        for half in range(2):
            x = lhs[block, half]
            cols = []
            for tile in range(2):
                at = pl.multiple_of((4 * block + 2 * half + tile) * LANES, LANES)
                pieces = []
                for piece in banded(interp[:, pl.ds(at, LANES)]):
                    pieces += [blank(32 * tile), piece] if tile else [piece]
                    pieces.append(blank(LANES - band_rows - 32 * tile))
                cols.append(jnp.concatenate(pieces, axis=0))
            fine = jnp.dot(
                jnp.concatenate([x, x], axis=1), jnp.concatenate(cols, axis=1), preferred_element_type=F32
            )
            for tile in range(2):
                at = pl.multiple_of((4 * block + 2 * half + tile) * LANES, LANES)
                sine, cosine = sin_cos(phase[:, pl.ds(at, LANES)])
                for pol in range(2):
                    re = fine[16 * pol:16 * pol + 8, tile * LANES:(tile + 1) * LANES]
                    im = fine[16 * pol + 8:16 * pol + 16, tile * LANES:(tile + 1) * LANES]
                    real.append(re * cosine - im * sine)
                    imag.append(re * sine + im * cosine)
        return jnp.concatenate([sublane_sums(real, sub), sublane_sums(imag, sub)], axis=0).astype(BF16)

    def post(block):
        for step in range(grp_size):
            grp = lax.rem(my_grp + step, grp_size)

            def away():
                pltpu.make_async_remote_copy(
                    src_ref=send.at[block], dst_ref=recv.at[me], send_sem=send_sem, recv_sem=recv_sem,
                    device_id=(grp, block), device_id_type=MESH,
                ).start()

            if step:
                away()
            else:
                pl.when(block != my_ang)(away)

                @pl.when(block == my_ang)
                def _():
                    pltpu.make_async_copy(send.at[block], recv.at[me], recv_sem).start()

    def blocks_of(step):
        return [lax.rem(my_ang + 1 + step * unroll + i, ang_size) for i in range(unroll)]

    def aggregate(step):
        for block in blocks_of(step):
            send[block] = one_block(block)

    def dispatch(step):
        for block in blocks_of(step):
            post(block)

    aggregate(0)
    pl.semaphore_wait(barrier, devices - 1)
    dispatch(0)

    def advance(step, carry):
        aggregate(step)
        dispatch(step)
        return carry

    lax.fori_loop(1, ang_size // unroll, advance, 0)

    for load in loads[4:]:
        load.wait()
    slots, clusters = sources.shape
    even = (sub & 1) == 0

    def pick(cluster, carry):
        for slot in range(slots):
            both = trans[trans_ids[slot, cluster]]
            both = both * jnp.where(slot < list_len[cluster], 1.0, 0.0)
            picked[cluster * slots + slot, 0] = jnp.where(even, both, pltpu.roll(both, 1, 0))
            picked[cluster * slots + slot, 1] = jnp.where(even, pltpu.roll(both, SUBS - 1, 0), both)
        return carry

    lax.fori_loop(0, clusters, pick, 0, unroll=2)

    pltpu.make_async_copy(recv, recv, recv_sem).wait()

    def widen(source, carry):
        patterns[source] = recv[source].astype(F32)
        return carry

    lax.fori_loop(0, devices, widen, 0, unroll=8)

    def receive(cluster, carry):
        real = imag = jnp.zeros((SUBS, LANES), F32)
        for slot in range(slots):
            source = sources[slot, cluster]
            row = cluster * slots + slot
            op_re, op_im = picked[row, 0], picked[row, 1]
            src_re, src_im = patterns[source, 0:SUBS], patterns[source, SUBS:2 * SUBS]
            real += op_re * src_re - op_im * src_im
            imag += op_re * src_im + op_im * src_re
        for part, value in enumerate((real, imag)):
            turned[cluster, part] = value
            for pol in range(2):
                out[part, cluster, 4 * pol:4 * pol + 4, :] = turned[cluster, part, pl.ds(pol, 4, stride=2), :]
        return carry

    lax.fori_loop(0, clusters, receive, 0, unroll=2)

    sent = recv.at[pl.ds(0, devices - 1)]
    pltpu.make_async_copy(sent, sent, send_sem).wait()


def local(grp_size, ang_size, children, present, interp, phase, trans, sources, trans_ids, list_len):
    parts, own, octants, pols, angles, coarse = children.shape
    operators, width = trans.shape[1:]
    clusters, slots = sources.shape
    devices = grp_size * ang_size
    quarters = width // LANES
    assert (parts, own, octants, pols, angles, quarters) == (2, 1, SUBS, 2, 1, 4)
    assert interp.shape[0] == SUBS and interp.shape[1] == ang_size * width == 4 * coarse
    children = children.reshape(parts * octants, pols, coarse)
    trans = trans.transpose(1, 0, 2).reshape(operators, parts, quarters, LANES)
    trans = trans.transpose(0, 2, 1, 3).reshape(operators, quarters * parts, LANES)
    operands = (children, present, interp, phase, trans, sources.T, trans_ids.T, list_len)
    tile_rows = 2 * SUBS
    received = pl.pallas_call(
        functools.partial(kernel, grp_size, ang_size, 4),
        out_shape=jax.ShapeDtypeStruct((parts, clusters, SUBS, LANES), F32),
        in_specs=[pl.BlockSpec(memory_space=pltpu.HBM)] * len(operands),
        out_specs=pl.BlockSpec(memory_space=pltpu.VMEM),
        scratch_shapes=[
            *(
                (pltpu.SMEM if operand.dtype == jnp.int32 else pltpu.VMEM)(operand.shape, operand.dtype)
                for operand in operands
            ),
            pltpu.VMEM((coarse // LANES, parts * octants * pols, LANES), F32),
            pltpu.VMEM((coarse // LANES, 2, parts * octants * pols, LANES), BF16),
            pltpu.VMEM((ang_size, tile_rows, LANES), BF16),
            pltpu.VMEM((devices, tile_rows, LANES), BF16),
            pltpu.VMEM((clusters * slots, 2, SUBS, LANES), F32),
            pltpu.VMEM((devices, tile_rows, LANES), F32),
            pltpu.VMEM((clusters, 2, SUBS, LANES), F32),
            pltpu.SemaphoreType.DMA((len(operands),)),
            pltpu.SemaphoreType.DMA,
            pltpu.SemaphoreType.DMA,
        ],
        compiler_params=pltpu.CompilerParams(
            collective_id=0, has_side_effects=True, vmem_limit_bytes=60 * 1024 * 1024
        ),
    )(*operands)
    return received.reshape(parts, clusters, pols, angles, width)


def solution(mesh):
    return jax.shard_map(
        functools.partial(local, mesh.shape["grp"], mesh.shape["ang"]),
        mesh=mesh,
        in_specs=(
            P(None, ("grp", "ang"), None, None, None, None),
            P(("grp", "ang"), None),
            P(),
            P(),
            P(None, None, "ang"),
            P("grp", None),
            P("grp", None),
            P("grp"),
        ),
        out_specs=P(None, "grp", None, None, "ang"),
        check_vma=False,
    )
```

```python
import functools

import jax
import jax.numpy as jnp
from jax import lax
from jax.experimental import pallas as pl
from jax.experimental.pallas import tpu as pltpu
from jax.sharding import PartitionSpec as P

MESH = pl.DeviceIdType.MESH
F32, BF16 = jnp.float32, jnp.bfloat16
LANES, SUBS = 128, 8

SIN_COEFFS = (0.999999996, -0.041666645, 0.000520815696, -3.09516959e-06, 1.01767836e-08)
COS_COEFFS = (0.999999953, -0.124999763, 0.00260397403, -2.1646421e-05, 9.04459312e-08)


def horner(coeffs, x):
    total = x * coeffs[-1] + coeffs[-2]
    for coeff in coeffs[-3::-1]:
        total = total * x + coeff
    return total


def sin_cos(angle):
    square = angle * angle
    twice_sine = angle * horner(SIN_COEFFS, square)
    return twice_sine * horner(COS_COEFFS, square), 1.0 - 0.5 * twice_sine * twice_sine


def iota(shape, axis):
    return lax.broadcasted_iota(jnp.int32, shape, axis)


def sublane_sums(rows, sub):
    low = (sub & 4) == 0
    rows = [
        jnp.where(low, rows[i], rows[i + 4]) + pltpu.roll(jnp.where(low, rows[i + 4], rows[i]), 4, 0)
        for i in range(4)
    ]
    for step in (2, 1):
        low = (sub & step) == 0
        rows = [
            jnp.where(low, rows[i], rows[i + step])
            + jnp.where(low, pltpu.roll(rows[i], SUBS - step, 0), pltpu.roll(rows[i + step], step, 0))
            for i in range(step)
        ]
    return rows[0]


def kernel(
    grp_size, ang_size, unroll,
    children_h, present_h, interp_h, phase_h, trans_h, sources_h, trans_ids_h, list_len_h,
    out,
    child_v, present, interp, phase, trans, sources, trans_ids, list_len, slabs, lhs, send, recv, picked, turned,
    load_sems, send_sem, recv_sem,
):
    my_grp, my_ang = lax.axis_index("grp"), lax.axis_index("ang")
    devices = grp_size * ang_size
    me = my_grp * ang_size + my_ang

    pairs = (
        (children_h, child_v), (present_h, present), (interp_h, interp), (phase_h, phase),
        (trans_h, trans), (sources_h, sources), (trans_ids_h, trans_ids), (list_len_h, list_len),
    )
    loads = [pltpu.make_async_copy(src, dst, load_sems.at[i]) for i, (src, dst) in enumerate(pairs)]
    for load in loads:
        load.start()

    barrier = pltpu.get_barrier_semaphore()

    def greet(step, carry):
        other = lax.rem(me + step, devices)
        pl.semaphore_signal(
            barrier, inc=1, device_id=(other // ang_size, lax.rem(other, ang_size)), device_id_type=MESH
        )
        return carry

    lax.fori_loop(1, devices, greet, 0)

    loads[0].wait()
    loads[1].wait()
    sub = iota((SUBS, LANES), 0)
    octants = present.shape[1]
    mask = jnp.zeros((SUBS, LANES), F32)
    for octant in range(octants):
        mask = jnp.where(sub == octant, present[0, octant].astype(F32), mask)

    coarse_tiles = slabs.shape[0]
    for tile in range(coarse_tiles):
        part = child_v[:, :, tile * LANES:(tile + 1) * LANES].astype(F32)
        for row in range(part.shape[0]):
            slabs[tile, 2 * row:2 * row + 2, :] = part[row]
    half_width = interp.shape[0] // 2
    lane = iota((SUBS, LANES), 1)

    def shifted(here, before, by):
        return jnp.where(lane < by, pltpu.roll(before, by, 1), pltpu.roll(here, by, 1))

    for pol in range(2):
        groups = []
        for reim in range(2):
            tiles = [
                slabs[tile, pl.ds(2 * octants * reim + pol, octants, stride=2), :] * mask
                for tile in range(coarse_tiles)
            ]
            groups.append(tiles)
        for tile in range(coarse_tiles):
            first = [shifted(g[tile], g[tile - 1], half_width) for g in groups]
            second = [
                shifted(g[(tile + 1) % coarse_tiles], g[tile], half_width + LANES // 2) for g in groups
            ]
            rows = slice(2 * octants * pol, 2 * octants * (pol + 1))
            lhs[tile, 0, rows, :] = jnp.concatenate(first, axis=0).astype(BF16)
            lhs[tile, 1, rows, :] = jnp.concatenate(second, axis=0).astype(BF16)

    loads[2].wait()
    loads[3].wait()

    band_rows = 48
    gap = iota((band_rows, LANES), 0) - iota((band_rows, LANES), 1) // 4
    band = jnp.where((gap >= 0) & (gap < SUBS), 1.0, 0.0).astype(BF16)
    turn = lane // 4

    def banded(weights):
        for step in (1, 2, 4):
            weights = jnp.where((turn & step) != 0, pltpu.roll(weights, step, 0), weights)
        high = weights.astype(BF16)
        low = (weights - high.astype(F32)).astype(BF16)
        return [jnp.concatenate([x] * (band_rows // SUBS), axis=0) * band for x in (high, low)]

    def blank(rows):
        return jnp.zeros((rows, LANES), BF16)

    def one_block(block):
        real, imag = [], []
        for half in range(2):
            x = lhs[block, half]
            cols = []
            for tile in range(2):
                at = pl.multiple_of((4 * block + 2 * half + tile) * LANES, LANES)
                pieces = []
                for piece in banded(interp[:, pl.ds(at, LANES)]):
                    pieces += [blank(32 * tile), piece] if tile else [piece]
                    pieces.append(blank(LANES - band_rows - 32 * tile))
                cols.append(jnp.concatenate(pieces, axis=0))
            fine = jnp.dot(
                jnp.concatenate([x, x], axis=1), jnp.concatenate(cols, axis=1), preferred_element_type=F32
            )
            for tile in range(2):
                at = pl.multiple_of((4 * block + 2 * half + tile) * LANES, LANES)
                sine, cosine = sin_cos(phase[:, pl.ds(at, LANES)])
                for pol in range(2):
                    re = fine[16 * pol:16 * pol + 8, tile * LANES:(tile + 1) * LANES]
                    im = fine[16 * pol + 8:16 * pol + 16, tile * LANES:(tile + 1) * LANES]
                    real.append(re * cosine - im * sine)
                    imag.append(re * sine + im * cosine)
        return jnp.concatenate([sublane_sums(real, sub), sublane_sums(imag, sub)], axis=0).astype(BF16)

    def post(block):
        for step in range(grp_size):
            grp = lax.rem(my_grp + step, grp_size)

            def away():
                pltpu.make_async_remote_copy(
                    src_ref=send.at[block], dst_ref=recv.at[me], send_sem=send_sem, recv_sem=recv_sem,
                    device_id=(grp, block), device_id_type=MESH,
                ).start()

            if step:
                away()
            else:
                pl.when(block != my_ang)(away)

                @pl.when(block == my_ang)
                def _():
                    pltpu.make_async_copy(send.at[block], recv.at[me], recv_sem).start()

    def blocks_of(step):
        return [lax.rem(my_ang + 1 + step * unroll + i, ang_size) for i in range(unroll)]

    def aggregate(step):
        for block in blocks_of(step):
            send[block] = one_block(block)

    def dispatch(step):
        for block in blocks_of(step):
            post(block)

    aggregate(0)
    pl.semaphore_wait(barrier, devices - 1)
    dispatch(0)

    def advance(step, carry):
        aggregate(step)
        dispatch(step)
        return carry

    lax.fori_loop(1, ang_size // unroll, advance, 0)

    for load in loads[4:]:
        load.wait()
    slots, clusters = sources.shape
    even = (sub & 1) == 0

    def pick(cluster, carry):
        for slot in range(slots):
            both = trans[trans_ids[slot, cluster]]
            both = both * jnp.where(slot < list_len[cluster], 1.0, 0.0)
            picked[cluster * slots + slot, 0] = jnp.where(even, both, pltpu.roll(both, 1, 0))
            picked[cluster * slots + slot, 1] = jnp.where(even, pltpu.roll(both, SUBS - 1, 0), both)
        return carry

    lax.fori_loop(0, clusters, pick, 0, unroll=2)

    pltpu.make_async_copy(recv, recv, recv_sem).wait()

    def receive(cluster, carry):
        real = imag = jnp.zeros((SUBS, LANES), F32)
        for slot in range(slots):
            source = sources[slot, cluster]
            row = cluster * slots + slot
            op_re, op_im = picked[row, 0], picked[row, 1]
            both = recv[source].astype(F32)
            src_re, src_im = both[0:SUBS], both[SUBS:2 * SUBS]
            real += op_re * src_re - op_im * src_im
            imag += op_re * src_im + op_im * src_re
        for part, value in enumerate((real, imag)):
            turned[cluster, part] = value
            for pol in range(2):
                out[part, cluster, 4 * pol:4 * pol + 4, :] = turned[cluster, part, pl.ds(pol, 4, stride=2), :]
        return carry

    lax.fori_loop(0, clusters, receive, 0, unroll=4)

    sent = recv.at[pl.ds(0, devices - 1)]
    pltpu.make_async_copy(sent, sent, send_sem).wait()


def local(grp_size, ang_size, children, present, interp, phase, trans, sources, trans_ids, list_len):
    parts, own, octants, pols, angles, coarse = children.shape
    operators, width = trans.shape[1:]
    clusters, slots = sources.shape
    devices = grp_size * ang_size
    quarters = width // LANES
    assert (parts, own, octants, pols, angles, quarters) == (2, 1, SUBS, 2, 1, 4)
    assert interp.shape[0] == SUBS and interp.shape[1] == ang_size * width == 4 * coarse
    children = children.reshape(parts * octants, pols, coarse)
    trans = trans.transpose(1, 0, 2).reshape(operators, parts, quarters, LANES)
    trans = trans.transpose(0, 2, 1, 3).reshape(operators, quarters * parts, LANES)
    operands = (children, present, interp, phase, trans, sources.T, trans_ids.T, list_len)
    tile_rows = 2 * SUBS
    operands = tuple(pltpu.with_memory_space_constraint(operand, pltpu.HBM) for operand in operands)
    received = pl.pallas_call(
        functools.partial(kernel, grp_size, ang_size, 4),
        out_shape=jax.ShapeDtypeStruct((parts, clusters, SUBS, LANES), F32),
        in_specs=[pl.BlockSpec(memory_space=pltpu.HBM)] * len(operands),
        out_specs=pl.BlockSpec(memory_space=pltpu.VMEM),
        scratch_shapes=[
            *(
                (pltpu.SMEM if operand.dtype == jnp.int32 else pltpu.VMEM)(operand.shape, operand.dtype)
                for operand in operands
            ),
            pltpu.VMEM((coarse // LANES, parts * octants * pols, LANES), F32),
            pltpu.VMEM((coarse // LANES, 2, parts * octants * pols, LANES), BF16),
            pltpu.VMEM((ang_size, tile_rows, LANES), BF16),
            pltpu.VMEM((devices, tile_rows, LANES), BF16),
            pltpu.VMEM((clusters * slots, 2, SUBS, LANES), F32),
            pltpu.VMEM((clusters, 2, SUBS, LANES), F32),
            pltpu.SemaphoreType.DMA((len(operands),)),
            pltpu.SemaphoreType.DMA,
            pltpu.SemaphoreType.DMA,
        ],
        compiler_params=pltpu.CompilerParams(
            collective_id=0, has_side_effects=True, vmem_limit_bytes=48 * 1024 * 1024
        ),
    )(*operands)
    return received.reshape(parts, clusters, pols, angles, width)


def solution(mesh):
    return jax.shard_map(
        functools.partial(local, mesh.shape["grp"], mesh.shape["ang"]),
        mesh=mesh,
        in_specs=(
            P(None, ("grp", "ang"), None, None, None, None),
            P(("grp", "ang"), None),
            P(),
            P(),
            P(None, None, "ang"),
            P("grp", None),
            P("grp", None),
            P("grp"),
        ),
        out_specs=P(None, "grp", None, None, "ang"),
        check_vma=False,
    )
```

```python
import functools

import jax
import jax.numpy as jnp
from jax import lax
from jax.experimental import pallas as pl
from jax.experimental.pallas import tpu as pltpu
from jax.sharding import PartitionSpec as P

MESH = pl.DeviceIdType.MESH
F32, BF16 = jnp.float32, jnp.bfloat16
LANES, SUBS = 128, 8
UNROLL = 2

SIN_COEFFS = (0.999999996, -0.041666645, 0.000520815696, -3.09516959e-06, 1.01767836e-08)
COS_COEFFS = (0.999999953, -0.124999763, 0.00260397403, -2.1646421e-05, 9.04459312e-08)


def horner(coeffs, x):
    total = x * coeffs[-1] + coeffs[-2]
    for coeff in coeffs[-3::-1]:
        total = total * x + coeff
    return total


def sin_cos(angle):
    square = angle * angle
    twice_sine = angle * horner(SIN_COEFFS, square)
    return twice_sine * horner(COS_COEFFS, square), 1.0 - 0.5 * twice_sine * twice_sine


def iota(shape, axis):
    return lax.broadcasted_iota(jnp.int32, shape, axis)


def sublane_sums(rows, sub):
    low = (sub & 4) == 0
    rows = [
        jnp.where(low, rows[i], rows[i + 4]) + pltpu.roll(jnp.where(low, rows[i + 4], rows[i]), 4, 0)
        for i in range(4)
    ]
    for step in (2, 1):
        low = (sub & step) == 0
        rows = [
            jnp.where(low, rows[i], rows[i + step])
            + jnp.where(low, pltpu.roll(rows[i], SUBS - step, 0), pltpu.roll(rows[i + step], step, 0))
            for i in range(step)
        ]
    return rows[0]


def kernel(
    grp_size, ang_size, unroll,
    children_h, present_h, interp_h, phase_h, trans_h, sources_h, trans_ids_h, list_len_h,
    out,
    child_v, present, interp, phase, trans, sources, trans_ids, list_len, slabs, lhs,
    stage_a, stage_b, send, recv, picked, turned,
    load_sems, send_sem, recv_sem,
):
    my_grp, my_ang = lax.axis_index("grp"), lax.axis_index("ang")
    devices = grp_size * ang_size
    me = my_grp * ang_size + my_ang

    pairs = (
        (children_h, child_v), (present_h, present), (interp_h, interp), (phase_h, phase),
        (trans_h, trans), (sources_h, sources), (trans_ids_h, trans_ids), (list_len_h, list_len),
    )
    loads = [pltpu.make_async_copy(src, dst, load_sems.at[i]) for i, (src, dst) in enumerate(pairs)]
    for load in loads:
        load.start()

    barrier = pltpu.get_barrier_semaphore()

    def greet(step, carry):
        other = lax.rem(me + step, devices)
        pl.semaphore_signal(
            barrier, inc=1, device_id=(other // ang_size, lax.rem(other, ang_size)), device_id_type=MESH
        )
        return carry

    lax.fori_loop(1, devices, greet, 0)

    loads[0].wait()
    loads[1].wait()
    sub = iota((SUBS, LANES), 0)
    octants = present.shape[1]
    mask = jnp.zeros((SUBS, LANES), F32)
    for octant in range(octants):
        mask = jnp.where(sub == octant, present[0, octant].astype(F32), mask)

    chunks = child_v.shape[0] // (2 * octants)
    chunk_tiles = child_v.shape[1] // 2
    coarse_tiles = chunks * chunk_tiles
    for row in range(child_v.shape[0]):
        slabs[row * 2 * chunk_tiles:(row + 1) * 2 * chunk_tiles, :] = child_v[row].astype(F32)
    half_width = interp.shape[0] // 2
    lane = iota((SUBS, LANES), 1)

    def shifted(here, before, by):
        return jnp.where(lane < by, pltpu.roll(before, by, 1), pltpu.roll(here, by, 1))

    for pol in range(2):
        groups = []
        for reim in range(2):
            tiles = [
                slabs[
                    pl.ds(
                        2 * chunk_tiles * (octants * chunks * reim + tile // chunk_tiles)
                        + 2 * (tile % chunk_tiles) + pol,
                        octants,
                        stride=2 * chunk_tiles * chunks,
                    ),
                    :,
                ] * mask
                for tile in range(coarse_tiles)
            ]
            groups.append(tiles)
        for tile in range(coarse_tiles):
            first = [shifted(g[tile], g[tile - 1], half_width) for g in groups]
            second = [
                shifted(g[(tile + 1) % coarse_tiles], g[tile], half_width + LANES // 2) for g in groups
            ]
            rows = slice(2 * octants * pol, 2 * octants * (pol + 1))
            lhs[tile, 0, rows, :] = jnp.concatenate(first, axis=0).astype(BF16)
            lhs[tile, 1, rows, :] = jnp.concatenate(second, axis=0).astype(BF16)

    loads[2].wait()
    loads[3].wait()

    band_rows = 48
    gap = iota((band_rows, LANES), 0) - iota((band_rows, LANES), 1) // 4
    band = jnp.where((gap >= 0) & (gap < SUBS), 1.0, 0.0).astype(BF16)
    turn = lane // 4

    def banded(weights):
        for step in (1, 2, 4):
            weights = jnp.where((turn & step) != 0, pltpu.roll(weights, step, 0), weights)
        high = weights.astype(BF16)
        low = (weights - high.astype(F32)).astype(BF16)
        return [jnp.concatenate([x] * (band_rows // SUBS), axis=0) * band for x in (high, low)]

    def blank(rows):
        return jnp.zeros((rows, LANES), BF16)

    def refine(block, stage):
        for half in range(2):
            x = lhs[block, half]
            cols = []
            for tile in range(2):
                at = pl.multiple_of((4 * block + 2 * half + tile) * LANES, LANES)
                pieces = []
                for piece in banded(interp[:, pl.ds(at, LANES)]):
                    pieces += [blank(32 * tile), piece] if tile else [piece]
                    pieces.append(blank(LANES - band_rows - 32 * tile))
                cols.append(jnp.concatenate(pieces, axis=0))
            stage[half] = jnp.dot(
                jnp.concatenate([x, x], axis=1), jnp.concatenate(cols, axis=1), preferred_element_type=F32
            )

    def combine(block, stage):
        real, imag = [], []
        for half in range(2):
            for tile in range(2):
                at = pl.multiple_of((4 * block + 2 * half + tile) * LANES, LANES)
                sine, cosine = sin_cos(phase[:, pl.ds(at, LANES)])
                cols = pl.ds(tile * LANES, LANES)
                for pol in range(2):
                    re = stage[half, 16 * pol:16 * pol + 8, cols]
                    im = stage[half, 16 * pol + 8:16 * pol + 16, cols]
                    real.append(re * cosine - im * sine)
                    imag.append(re * sine + im * cosine)
        send[block] = jnp.concatenate(
            [sublane_sums(real, sub), sublane_sums(imag, sub)], axis=0
        ).astype(BF16)

    def post(block, own):
        for step in range(grp_size):
            if own and not step:
                pltpu.make_async_copy(send.at[block], recv.at[me], recv_sem).start()
                continue
            pltpu.make_async_remote_copy(
                src_ref=send.at[block], dst_ref=recv.at[me], send_sem=send_sem, recv_sem=recv_sem,
                device_id=(lax.rem(my_grp + step, grp_size), block), device_id_type=MESH,
            ).start()

    def block_at(step):
        return lax.rem(my_ang + 1 + step, ang_size)

    def refine_group(group, stages):
        for i in range(unroll):
            refine(block_at(group * unroll + i), stages.at[i])

    def combine_group(group, stages, last=False):
        for i in range(unroll):
            combine(block_at(group * unroll + i), stages.at[i])
        for i in range(unroll):
            post(block_at(group * unroll + i), last and i == unroll - 1)

    refine_group(0, stage_a)
    pl.semaphore_wait(barrier, devices - 1)
    rounds = ang_size // (2 * unroll)

    def advance(step, carry):
        refine_group(2 * step + 1, stage_b)
        combine_group(2 * step, stage_a)
        refine_group(2 * step + 2, stage_a)
        combine_group(2 * step + 1, stage_b)
        return carry

    lax.fori_loop(0, rounds - 1, advance, 0)
    refine_group(2 * rounds - 1, stage_b)
    combine_group(2 * rounds - 2, stage_a)
    combine_group(2 * rounds - 1, stage_b, last=True)

    for load in loads[4:]:
        load.wait()
    slots, clusters = sources.shape
    even = (sub & 1) == 0

    def pick(cluster, carry):
        for slot in range(slots):
            both = trans[trans_ids[slot, cluster]]
            both = both * jnp.where(slot < list_len[cluster], 1.0, 0.0)
            picked[cluster * slots + slot, 0] = jnp.where(even, both, pltpu.roll(both, 1, 0))
            picked[cluster * slots + slot, 1] = jnp.where(even, pltpu.roll(both, SUBS - 1, 0), both)
        return carry

    lax.fori_loop(0, clusters, pick, 0, unroll=2)

    pltpu.make_async_copy(recv, recv, recv_sem).wait()

    def receive(cluster, carry):
        real = imag = jnp.zeros((SUBS, LANES), F32)
        for slot in range(slots):
            source = sources[slot, cluster]
            row = cluster * slots + slot
            op_re, op_im = picked[row, 0], picked[row, 1]
            both = recv[source].astype(F32)
            src_re, src_im = both[0:SUBS], both[SUBS:2 * SUBS]
            real += op_re * src_re - op_im * src_im
            imag += op_re * src_im + op_im * src_re
        for part, value in enumerate((real, imag)):
            turned[cluster, part] = value
            for pol in range(2):
                out[part, cluster, 4 * pol:4 * pol + 4, :] = turned[cluster, part, pl.ds(pol, 4, stride=2), :]
        return carry

    lax.fori_loop(0, clusters, receive, 0, unroll=4)

    sent = recv.at[pl.ds(0, devices - 1)]
    pltpu.make_async_copy(sent, sent, send_sem).wait()


def local(grp_size, ang_size, children, present, interp, phase, trans, sources, trans_ids, list_len):
    parts, own, octants, pols, angles, coarse = children.shape
    operators, width = trans.shape[1:]
    clusters, slots = sources.shape
    assert ang_size % (2 * UNROLL) == 0
    devices = grp_size * ang_size
    quarters = width // LANES
    assert (parts, own, octants, pols, angles, quarters) == (2, 1, SUBS, 2, 1, 4)
    assert interp.shape[0] == SUBS and interp.shape[1] == ang_size * width == 4 * coarse
    chunk = SUBS * LANES
    children = children.reshape(parts * octants, pols, coarse // chunk, SUBS, LANES)
    children = children.transpose(0, 2, 3, 1, 4).reshape(parts * octants * coarse // chunk, 2 * SUBS, LANES)
    trans = trans.transpose(1, 0, 2).reshape(operators, parts, quarters, LANES)
    trans = trans.transpose(0, 2, 1, 3).reshape(operators, quarters * parts, LANES)
    operands = (children, present, interp, phase, trans, sources.T, trans_ids.T, list_len)
    tile_rows = 2 * SUBS
    operands = tuple(pltpu.with_memory_space_constraint(operand, pltpu.HBM) for operand in operands)
    received = pl.pallas_call(
        functools.partial(kernel, grp_size, ang_size, UNROLL),
        out_shape=jax.ShapeDtypeStruct((parts, clusters, SUBS, LANES), F32),
        in_specs=[pl.BlockSpec(memory_space=pltpu.HBM)] * len(operands),
        out_specs=pl.BlockSpec(memory_space=pltpu.VMEM),
        scratch_shapes=[
            *(
                (pltpu.SMEM if operand.dtype == jnp.int32 else pltpu.VMEM)(operand.shape, operand.dtype)
                for operand in operands
            ),
            pltpu.VMEM((children.size // LANES, LANES), F32),
            pltpu.VMEM((coarse // LANES, 2, parts * octants * pols, LANES), BF16),
            pltpu.VMEM((UNROLL, 2, parts * octants * pols, 2 * LANES), F32),
            pltpu.VMEM((UNROLL, 2, parts * octants * pols, 2 * LANES), F32),
            pltpu.VMEM((ang_size, tile_rows, LANES), BF16),
            pltpu.VMEM((devices, tile_rows, LANES), BF16),
            pltpu.VMEM((clusters * slots, 2, SUBS, LANES), F32),
            pltpu.VMEM((clusters, 2, SUBS, LANES), F32),
            pltpu.SemaphoreType.DMA((len(operands),)),
            pltpu.SemaphoreType.DMA,
            pltpu.SemaphoreType.DMA,
        ],
        compiler_params=pltpu.CompilerParams(
            collective_id=0, has_side_effects=True, vmem_limit_bytes=48 * 1024 * 1024
        ),
    )(*operands)
    return received.reshape(parts, clusters, pols, angles, width)


def solution(mesh):
    return jax.shard_map(
        functools.partial(local, mesh.shape["grp"], mesh.shape["ang"]),
        mesh=mesh,
        in_specs=(
            P(None, ("grp", "ang"), None, None, None, None),
            P(("grp", "ang"), None),
            P(),
            P(),
            P(None, None, "ang"),
            P("grp", None),
            P("grp", None),
            P("grp"),
        ),
        out_specs=P(None, "grp", None, None, "ang"),
        check_vma=False,
    )
```

```python
import functools

import jax
import jax.numpy as jnp
from jax import lax
from jax.experimental import pallas as pl
from jax.experimental.pallas import tpu as pltpu
from jax.sharding import PartitionSpec as P

MESH = pl.DeviceIdType.MESH
F32, BF16 = jnp.float32, jnp.bfloat16
LANES, SUBS = 128, 8
UNROLL = 4

SIN_COEFFS = (0.999999996, -0.041666645, 0.000520815696, -3.09516959e-06, 1.01767836e-08)
COS_COEFFS = (0.999999953, -0.124999763, 0.00260397403, -2.1646421e-05, 9.04459312e-08)


def horner(coeffs, x):
    total = x * coeffs[-1] + coeffs[-2]
    for coeff in coeffs[-3::-1]:
        total = total * x + coeff
    return total


def sin_cos(angle):
    square = angle * angle
    twice_sine = angle * horner(SIN_COEFFS, square)
    return twice_sine * horner(COS_COEFFS, square), 1.0 - 0.5 * twice_sine * twice_sine


def iota(shape, axis):
    return lax.broadcasted_iota(jnp.int32, shape, axis)


def sublane_sums(rows, sub):
    low = (sub & 4) == 0
    rows = [
        jnp.where(low, rows[i], rows[i + 4]) + pltpu.roll(jnp.where(low, rows[i + 4], rows[i]), 4, 0)
        for i in range(4)
    ]
    for step in (2, 1):
        low = (sub & step) == 0
        rows = [
            jnp.where(low, rows[i], rows[i + step])
            + jnp.where(low, pltpu.roll(rows[i], SUBS - step, 0), pltpu.roll(rows[i + step], step, 0))
            for i in range(step)
        ]
    return rows[0]


def kernel(
    grp_size, ang_size, unroll,
    children_h, present_h, interp_h, phase_h, trans_h, sources_h, trans_ids_h, list_len_h,
    out,
    child_v, present, interp, phase, trans, sources, trans_ids, list_len, slabs, lhs,
    stage_a, stage_b, send, recv, picked, turned,
    load_sems, send_sem, recv_sem,
):
    my_grp, my_ang = lax.axis_index("grp"), lax.axis_index("ang")
    devices = grp_size * ang_size
    me = my_grp * ang_size + my_ang

    def wrap(index, size):
        return jnp.where(index >= size, index - size, index)

    def grp_at(step):
        return wrap(my_grp + step, grp_size)

    def ang_at(step):
        return wrap(my_ang + step, ang_size)

    pairs = (
        (children_h, child_v), (present_h, present), (interp_h, interp), (phase_h, phase),
        (trans_h, trans), (sources_h, sources), (trans_ids_h, trans_ids), (list_len_h, list_len),
    )
    loads = [pltpu.make_async_copy(src, dst, load_sems.at[i]) for i, (src, dst) in enumerate(pairs)]
    for load in loads:
        load.start()

    barrier = pltpu.get_barrier_semaphore()

    for grp_step in range(grp_size):
        for ang_step in range(ang_size):
            if grp_step or ang_step:
                pl.semaphore_signal(
                    barrier, inc=1, device_id=(grp_at(grp_step), ang_at(ang_step)), device_id_type=MESH
                )

    loads[0].wait()
    loads[1].wait()
    sub = iota((SUBS, LANES), 0)
    octants = present.shape[1]
    mask = jnp.zeros((SUBS, LANES), F32)
    for octant in range(octants):
        mask = jnp.where(sub == octant, present[0, octant].astype(F32), mask)

    chunks = child_v.shape[0] // (2 * octants)
    chunk_tiles = child_v.shape[1] // 2
    coarse_tiles = chunks * chunk_tiles
    for row in range(child_v.shape[0]):
        slabs[row * 2 * chunk_tiles:(row + 1) * 2 * chunk_tiles, :] = child_v[row].astype(F32)
    half_width = interp.shape[0] // 2
    lane = iota((SUBS, LANES), 1)

    def shifted(here, before, by):
        return jnp.where(lane < by, pltpu.roll(before, by, 1), pltpu.roll(here, by, 1))

    for pol in range(2):
        groups = []
        for reim in range(2):
            tiles = [
                slabs[
                    pl.ds(
                        2 * chunk_tiles * (octants * chunks * reim + tile // chunk_tiles)
                        + 2 * (tile % chunk_tiles) + pol,
                        octants,
                        stride=2 * chunk_tiles * chunks,
                    ),
                    :,
                ] * mask
                for tile in range(coarse_tiles)
            ]
            groups.append(tiles)
        for tile in range(coarse_tiles):
            first = [shifted(g[tile], g[tile - 1], half_width) for g in groups]
            second = [
                shifted(g[(tile + 1) % coarse_tiles], g[tile], half_width + LANES // 2) for g in groups
            ]
            rows = slice(2 * octants * pol, 2 * octants * (pol + 1))
            lhs[tile, 0, rows, :] = jnp.concatenate(first, axis=0).astype(BF16)
            lhs[tile, 1, rows, :] = jnp.concatenate(second, axis=0).astype(BF16)

    loads[2].wait()
    loads[3].wait()

    band_rows = 48
    gap = iota((band_rows, LANES), 0) - iota((band_rows, LANES), 1) // 4
    band = jnp.where((gap >= 0) & (gap < SUBS), 1.0, 0.0).astype(BF16)
    turn = lane // 4

    def banded(weights):
        for step in (1, 2, 4):
            weights = jnp.where((turn & step) != 0, pltpu.roll(weights, step, 0), weights)
        high = weights.astype(BF16)
        low = (weights - high.astype(F32)).astype(BF16)
        return [jnp.concatenate([x] * (band_rows // SUBS), axis=0) * band for x in (high, low)]

    def blank(rows):
        return jnp.zeros((rows, LANES), BF16)

    def refine(block, stage):
        for half in range(2):
            x = lhs[block, half]
            cols = []
            for tile in range(2):
                at = pl.multiple_of((4 * block + 2 * half + tile) * LANES, LANES)
                pieces = []
                for piece in banded(interp[:, pl.ds(at, LANES)]):
                    pieces += [blank(32 * tile), piece] if tile else [piece]
                    pieces.append(blank(LANES - band_rows - 32 * tile))
                cols.append(jnp.concatenate(pieces, axis=0))
            stage[half] = jnp.dot(
                jnp.concatenate([x, x], axis=1), jnp.concatenate(cols, axis=1), preferred_element_type=F32
            )

    def combine(block, stage):
        real, imag = [], []
        for half in range(2):
            for tile in range(2):
                at = pl.multiple_of((4 * block + 2 * half + tile) * LANES, LANES)
                sine, cosine = sin_cos(phase[:, pl.ds(at, LANES)])
                cols = pl.ds(tile * LANES, LANES)
                for pol in range(2):
                    re = stage[half, 16 * pol:16 * pol + 8, cols]
                    im = stage[half, 16 * pol + 8:16 * pol + 16, cols]
                    real.append(re * cosine - im * sine)
                    imag.append(re * sine + im * cosine)
        send[block] = jnp.concatenate(
            [sublane_sums(real, sub), sublane_sums(imag, sub)], axis=0
        ).astype(BF16)

    def post(block, own):
        for step in range(grp_size):
            if own and not step:
                pltpu.make_async_copy(send.at[block], recv.at[me], recv_sem).start()
                continue
            pltpu.make_async_remote_copy(
                src_ref=send.at[block], dst_ref=recv.at[me], send_sem=send_sem, recv_sem=recv_sem,
                device_id=(grp_at(step), block), device_id_type=MESH,
            ).start()

    def block_at(step):
        return ang_at(1 + step)

    def refine_group(group, stages):
        for i in range(unroll):
            refine(block_at(group * unroll + i), stages.at[i])

    def combine_group(group, stages):
        for i in range(unroll):
            combine(block_at(group * unroll + i), stages.at[i])

    def post_group(group, last=False):
        for i in range(unroll):
            post(block_at(group * unroll + i), last and i == unroll - 1)

    def one_round(step, last=False):
        refine_group(2 * step + 1, stage_b)
        combine_group(2 * step, stage_a)
        if isinstance(step, int) and step == 0:
            pl.semaphore_wait(barrier, devices - 1)
        post_group(2 * step)
        if not last:
            refine_group(2 * step + 2, stage_a)
        combine_group(2 * step + 1, stage_b)
        post_group(2 * step + 1, last)

    def advance(step, carry):
        one_round(step)
        return carry

    refine_group(0, stage_a)
    rounds = ang_size // (2 * unroll)
    one_round(0, rounds == 1)
    if rounds > 2:
        lax.fori_loop(1, rounds - 1, advance, 0)
    if rounds > 1:
        one_round(rounds - 1, True)

    for load in loads[4:]:
        load.wait()
    slots, clusters = sources.shape
    even = (sub & 1) == 0

    def pick(cluster, carry):
        for slot in range(slots):
            both = trans[trans_ids[slot, cluster]]
            both = both * jnp.where(slot < list_len[cluster], 1.0, 0.0)
            picked[cluster * slots + slot, 0] = jnp.where(even, both, pltpu.roll(both, 1, 0))
            picked[cluster * slots + slot, 1] = jnp.where(even, pltpu.roll(both, SUBS - 1, 0), both)
        return carry

    lax.fori_loop(0, clusters, pick, 0, unroll=2)

    pltpu.make_async_copy(recv, recv, recv_sem).wait()

    def receive(cluster, carry):
        real = imag = jnp.zeros((SUBS, LANES), F32)
        for slot in range(slots):
            source = sources[slot, cluster]
            row = cluster * slots + slot
            op_re, op_im = picked[row, 0], picked[row, 1]
            both = recv[source].astype(F32)
            src_re, src_im = both[0:SUBS], both[SUBS:2 * SUBS]
            real += op_re * src_re - op_im * src_im
            imag += op_re * src_im + op_im * src_re
        for part, value in enumerate((real, imag)):
            turned[cluster, part] = value
            for pol in range(2):
                out[part, cluster, 4 * pol:4 * pol + 4, :] = turned[cluster, part, pl.ds(pol, 4, stride=2), :]
        return carry

    lax.fori_loop(0, clusters, receive, 0, unroll=4)

    sent = recv.at[pl.ds(0, devices - 1)]
    pltpu.make_async_copy(sent, sent, send_sem).wait()


def local(grp_size, ang_size, children, present, interp, phase, trans, sources, trans_ids, list_len):
    parts, own, octants, pols, angles, coarse = children.shape
    operators, width = trans.shape[1:]
    clusters, slots = sources.shape
    assert ang_size % (2 * UNROLL) == 0
    devices = grp_size * ang_size
    quarters = width // LANES
    assert (parts, own, octants, pols, angles, quarters) == (2, 1, SUBS, 2, 1, 4)
    assert interp.shape[0] == SUBS and interp.shape[1] == ang_size * width == 4 * coarse
    chunk = SUBS * LANES
    children = children.reshape(parts * octants, pols, coarse // chunk, SUBS, LANES)
    children = children.transpose(0, 2, 3, 1, 4).reshape(parts * octants * coarse // chunk, 2 * SUBS, LANES)
    trans = trans.transpose(1, 0, 2).reshape(operators, parts, quarters, LANES)
    trans = trans.transpose(0, 2, 1, 3).reshape(operators, quarters * parts, LANES)
    operands = (children, present, interp, phase, trans, sources.T, trans_ids.T, list_len)
    tile_rows = 2 * SUBS
    operands = tuple(pltpu.with_memory_space_constraint(operand, pltpu.HBM) for operand in operands)
    received = pl.pallas_call(
        functools.partial(kernel, grp_size, ang_size, UNROLL),
        out_shape=jax.ShapeDtypeStruct((parts, clusters, SUBS, LANES), F32),
        in_specs=[pl.BlockSpec(memory_space=pltpu.HBM)] * len(operands),
        out_specs=pl.BlockSpec(memory_space=pltpu.VMEM),
        scratch_shapes=[
            *(
                (pltpu.SMEM if operand.dtype == jnp.int32 else pltpu.VMEM)(operand.shape, operand.dtype)
                for operand in operands
            ),
            pltpu.VMEM((children.size // LANES, LANES), F32),
            pltpu.VMEM((coarse // LANES, 2, parts * octants * pols, LANES), BF16),
            pltpu.VMEM((UNROLL, 2, parts * octants * pols, 2 * LANES), F32),
            pltpu.VMEM((UNROLL, 2, parts * octants * pols, 2 * LANES), F32),
            pltpu.VMEM((ang_size, tile_rows, LANES), BF16),
            pltpu.VMEM((devices, tile_rows, LANES), BF16),
            pltpu.VMEM((clusters * slots, 2, SUBS, LANES), F32),
            pltpu.VMEM((clusters, 2, SUBS, LANES), F32),
            pltpu.SemaphoreType.DMA((len(operands),)),
            pltpu.SemaphoreType.DMA,
            pltpu.SemaphoreType.DMA,
        ],
        compiler_params=pltpu.CompilerParams(
            collective_id=0, has_side_effects=True, vmem_limit_bytes=48 * 1024 * 1024
        ),
    )(*operands)
    return received.reshape(parts, clusters, pols, angles, width)


def solution(mesh):
    return jax.shard_map(
        functools.partial(local, mesh.shape["grp"], mesh.shape["ang"]),
        mesh=mesh,
        in_specs=(
            P(None, ("grp", "ang"), None, None, None, None),
            P(("grp", "ang"), None),
            P(),
            P(),
            P(None, None, "ang"),
            P("grp", None),
            P("grp", None),
            P("grp"),
        ),
        out_specs=P(None, "grp", None, None, "ang"),
        check_vma=False,
    )
```

```python
import functools

import jax
import jax.numpy as jnp
from jax import lax
from jax.experimental import pallas as pl
from jax.experimental.pallas import tpu as pltpu
from jax.sharding import PartitionSpec as P

MESH = pl.DeviceIdType.MESH
F32, BF16 = jnp.float32, jnp.bfloat16
LANES, SUBS = 128, 8
UNROLL = 4

SIN_COEFFS = (0.999999996, -0.041666645, 0.000520815696, -3.09516959e-06, 1.01767836e-08)
COS_COEFFS = (0.999999953, -0.124999763, 0.00260397403, -2.1646421e-05, 9.04459312e-08)


def horner(coeffs, x):
    total = x * coeffs[-1] + coeffs[-2]
    for coeff in coeffs[-3::-1]:
        total = total * x + coeff
    return total


def sin_cos(angle):
    square = angle * angle
    twice_sine = angle * horner(SIN_COEFFS, square)
    return twice_sine * horner(COS_COEFFS, square), 1.0 - 0.5 * twice_sine * twice_sine


def iota(shape, axis):
    return lax.broadcasted_iota(jnp.int32, shape, axis)


def sublane_sums(rows, sub):
    low = (sub & 4) == 0
    rows = [
        jnp.where(low, rows[i], rows[i + 4]) + pltpu.roll(jnp.where(low, rows[i + 4], rows[i]), 4, 0)
        for i in range(4)
    ]
    for step in (2, 1):
        low = (sub & step) == 0
        rows = [
            jnp.where(low, rows[i], rows[i + step])
            + jnp.where(low, pltpu.roll(rows[i], SUBS - step, 0), pltpu.roll(rows[i + step], step, 0))
            for i in range(step)
        ]
    return rows[0]


def kernel(
    grp_size, ang_size, unroll,
    children_h, present_h, interp_h, phase_h, trans_h, sources_h, trans_ids_h, list_len_h,
    out,
    child_v, present, interp, phase, trans, sources, trans_ids, list_len, slabs, lhs,
    stage_a, stage_b, send, recv, picked, turned,
    load_sems, send_sem, recv_sem,
):
    my_grp, my_ang = lax.axis_index("grp"), lax.axis_index("ang")
    devices = grp_size * ang_size
    me = my_grp * ang_size + my_ang

    def wrap(index, size):
        return jnp.where(index >= size, index - size, index)

    def grp_at(step):
        return wrap(my_grp + step, grp_size)

    def ang_at(step):
        return wrap(my_ang + step, ang_size)

    pairs = (
        (children_h, child_v), (present_h, present), (interp_h, interp), (phase_h, phase),
        (trans_h, trans), (sources_h, sources), (trans_ids_h, trans_ids), (list_len_h, list_len),
    )
    loads = [pltpu.make_async_copy(src, dst, load_sems.at[i]) for i, (src, dst) in enumerate(pairs)]
    for load in loads:
        load.start()

    barrier = pltpu.get_barrier_semaphore()

    for grp_step in range(grp_size):
        for ang_step in range(ang_size):
            if grp_step or ang_step:
                pl.semaphore_signal(
                    barrier, inc=1, device_id=(grp_at(grp_step), ang_at(ang_step)), device_id_type=MESH
                )

    loads[0].wait()
    loads[1].wait()
    sub = iota((SUBS, LANES), 0)
    octants = present.shape[1]
    mask = jnp.zeros((SUBS, LANES), F32)
    for octant in range(octants):
        mask = jnp.where(sub == octant, present[0, octant].astype(F32), mask)

    chunks = child_v.shape[0] // (2 * octants)
    chunk_tiles = child_v.shape[1] // 2
    coarse_tiles = chunks * chunk_tiles
    for row in range(child_v.shape[0]):
        slabs[row * 2 * chunk_tiles:(row + 1) * 2 * chunk_tiles, :] = child_v[row].astype(F32)
    half_width = interp.shape[0] // 2
    lane = iota((SUBS, LANES), 1)

    def shifted(here, before, by):
        return jnp.where(lane < by, pltpu.roll(before, by, 1), pltpu.roll(here, by, 1))

    for pol in range(2):
        groups = []
        for reim in range(2):
            tiles = [
                slabs[
                    pl.ds(
                        2 * chunk_tiles * (octants * chunks * reim + tile // chunk_tiles)
                        + 2 * (tile % chunk_tiles) + pol,
                        octants,
                        stride=2 * chunk_tiles * chunks,
                    ),
                    :,
                ] * mask
                for tile in range(coarse_tiles)
            ]
            groups.append(tiles)
        for tile in range(coarse_tiles):
            first = [shifted(g[tile], g[tile - 1], half_width) for g in groups]
            second = [
                shifted(g[(tile + 1) % coarse_tiles], g[tile], half_width + LANES // 2) for g in groups
            ]
            rows = slice(2 * octants * pol, 2 * octants * (pol + 1))
            lhs[tile, 0, rows, :] = jnp.concatenate(first, axis=0).astype(BF16)
            lhs[tile, 1, rows, :] = jnp.concatenate(second, axis=0).astype(BF16)

    loads[2].wait()
    loads[3].wait()

    band_rows = 48
    gap = iota((band_rows, LANES), 0) - iota((band_rows, LANES), 1) // 4
    band = jnp.where((gap >= 0) & (gap < SUBS), 1.0, 0.0).astype(BF16)
    turn = lane // 4

    def banded(weights):
        for step in (1, 2, 4):
            weights = jnp.where((turn & step) != 0, pltpu.roll(weights, step, 0), weights)
        high = weights.astype(BF16)
        low = (weights - high.astype(F32)).astype(BF16)
        return [jnp.concatenate([x] * (band_rows // SUBS), axis=0) * band for x in (high, low)]

    def blank(rows):
        return jnp.zeros((rows, LANES), BF16)

    def refine(block, stage):
        for half in range(2):
            x = lhs[block, half]
            cols = []
            for tile in range(2):
                at = pl.multiple_of((4 * block + 2 * half + tile) * LANES, LANES)
                pieces = []
                for piece in banded(interp[:, pl.ds(at, LANES)]):
                    pieces += [blank(32 * tile), piece] if tile else [piece]
                    pieces.append(blank(LANES - band_rows - 32 * tile))
                cols.append(jnp.concatenate(pieces, axis=0))
            stage[half] = jnp.dot(
                jnp.concatenate([x, x], axis=1), jnp.concatenate(cols, axis=1), preferred_element_type=F32
            )

    def combine(block, stage):
        real, imag = [], []
        for half in range(2):
            for tile in range(2):
                at = pl.multiple_of((4 * block + 2 * half + tile) * LANES, LANES)
                sine, cosine = sin_cos(phase[:, pl.ds(at, LANES)])
                cols = pl.ds(tile * LANES, LANES)
                for pol in range(2):
                    re = stage[half, 16 * pol:16 * pol + 8, cols]
                    im = stage[half, 16 * pol + 8:16 * pol + 16, cols]
                    real.append(re * cosine - im * sine)
                    imag.append(re * sine + im * cosine)
        send[block] = jnp.concatenate(
            [sublane_sums(real, sub), sublane_sums(imag, sub)], axis=0
        ).astype(BF16)

    def post(block, own):
        for step in range(grp_size):
            if own and not step:
                pltpu.make_async_copy(send.at[block], recv.at[me], recv_sem).start()
                continue
            pltpu.make_async_remote_copy(
                src_ref=send.at[block], dst_ref=recv.at[me], send_sem=send_sem, recv_sem=recv_sem,
                device_id=(grp_at(step), block), device_id_type=MESH,
            ).start()

    def block_at(step):
        code = ang_size - 1 - step
        weight, block = 1, 0
        while weight < ang_size:
            digit = lax.rem(code // weight + lax.div(my_ang, weight), 2)
            block, weight = block + digit * weight, 2 * weight
        return block

    def refine_group(group, stages):
        for i in range(unroll):
            refine(block_at(group * unroll + i), stages.at[i])

    def combine_group(group, stages):
        for i in range(unroll):
            combine(block_at(group * unroll + i), stages.at[i])

    def post_group(group, last=False):
        for i in range(unroll):
            post(block_at(group * unroll + i), last and i == unroll - 1)

    def one_round(step, last=False):
        refine_group(2 * step + 1, stage_b)
        combine_group(2 * step, stage_a)
        if isinstance(step, int) and step == 0:
            pl.semaphore_wait(barrier, devices - 1)
        post_group(2 * step)
        if not last:
            refine_group(2 * step + 2, stage_a)
        combine_group(2 * step + 1, stage_b)
        post_group(2 * step + 1, last)

    def advance(step, carry):
        one_round(step)
        return carry

    refine_group(0, stage_a)
    rounds = ang_size // (2 * unroll)
    one_round(0, rounds == 1)
    if rounds > 2:
        lax.fori_loop(1, rounds - 1, advance, 0)
    if rounds > 1:
        one_round(rounds - 1, True)

    for load in loads[4:]:
        load.wait()
    slots, clusters = sources.shape
    even = (sub & 1) == 0

    def pick(cluster, carry):
        for slot in range(slots):
            both = trans[trans_ids[slot, cluster]]
            both = both * jnp.where(slot < list_len[cluster], 1.0, 0.0)
            picked[cluster * slots + slot, 0] = jnp.where(even, both, pltpu.roll(both, 1, 0))
            picked[cluster * slots + slot, 1] = jnp.where(even, pltpu.roll(both, SUBS - 1, 0), both)
        return carry

    lax.fori_loop(0, clusters, pick, 0, unroll=2)

    pltpu.make_async_copy(recv, recv, recv_sem).wait()

    def receive(cluster, carry):
        real = imag = jnp.zeros((SUBS, LANES), F32)
        for slot in range(slots):
            source = sources[slot, cluster]
            row = cluster * slots + slot
            op_re, op_im = picked[row, 0], picked[row, 1]
            both = recv[source].astype(F32)
            src_re, src_im = both[0:SUBS], both[SUBS:2 * SUBS]
            real += op_re * src_re - op_im * src_im
            imag += op_re * src_im + op_im * src_re
        for part, value in enumerate((real, imag)):
            turned[cluster, part] = value
            for pol in range(2):
                out[part, cluster, 4 * pol:4 * pol + 4, :] = turned[cluster, part, pl.ds(pol, 4, stride=2), :]
        return carry

    lax.fori_loop(0, clusters, receive, 0, unroll=4)

    sent = recv.at[pl.ds(0, devices - 1)]
    pltpu.make_async_copy(sent, sent, send_sem).wait()


def local(grp_size, ang_size, children, present, interp, phase, trans, sources, trans_ids, list_len):
    parts, own, octants, pols, angles, coarse = children.shape
    operators, width = trans.shape[1:]
    clusters, slots = sources.shape
    assert ang_size % (2 * UNROLL) == 0 and ang_size & (ang_size - 1) == 0
    devices = grp_size * ang_size
    quarters = width // LANES
    assert (parts, own, octants, pols, angles, quarters) == (2, 1, SUBS, 2, 1, 4)
    assert interp.shape[0] == SUBS and interp.shape[1] == ang_size * width == 4 * coarse
    chunk = SUBS * LANES
    children = children.reshape(parts * octants, pols, coarse // chunk, SUBS, LANES)
    children = children.transpose(0, 2, 3, 1, 4).reshape(parts * octants * coarse // chunk, 2 * SUBS, LANES)
    trans = trans.transpose(1, 0, 2).reshape(operators, parts, quarters, LANES)
    trans = trans.transpose(0, 2, 1, 3).reshape(operators, quarters * parts, LANES)
    operands = (children, present, interp, phase, trans, sources.T, trans_ids.T, list_len)
    tile_rows = 2 * SUBS
    operands = tuple(pltpu.with_memory_space_constraint(operand, pltpu.HBM) for operand in operands)
    received = pl.pallas_call(
        functools.partial(kernel, grp_size, ang_size, UNROLL),
        out_shape=jax.ShapeDtypeStruct((parts, clusters, SUBS, LANES), F32),
        in_specs=[pl.BlockSpec(memory_space=pltpu.HBM)] * len(operands),
        out_specs=pl.BlockSpec(memory_space=pltpu.VMEM),
        scratch_shapes=[
            *(
                (pltpu.SMEM if operand.dtype == jnp.int32 else pltpu.VMEM)(operand.shape, operand.dtype)
                for operand in operands
            ),
            pltpu.VMEM((children.size // LANES, LANES), F32),
            pltpu.VMEM((coarse // LANES, 2, parts * octants * pols, LANES), BF16),
            pltpu.VMEM((UNROLL, 2, parts * octants * pols, 2 * LANES), F32),
            pltpu.VMEM((UNROLL, 2, parts * octants * pols, 2 * LANES), F32),
            pltpu.VMEM((ang_size, tile_rows, LANES), BF16),
            pltpu.VMEM((devices, tile_rows, LANES), BF16),
            pltpu.VMEM((clusters * slots, 2, SUBS, LANES), F32),
            pltpu.VMEM((clusters, 2, SUBS, LANES), F32),
            pltpu.SemaphoreType.DMA((len(operands),)),
            pltpu.SemaphoreType.DMA,
            pltpu.SemaphoreType.DMA,
        ],
        compiler_params=pltpu.CompilerParams(
            collective_id=0, has_side_effects=True, vmem_limit_bytes=48 * 1024 * 1024
        ),
    )(*operands)
    return received.reshape(parts, clusters, pols, angles, width)


def solution(mesh):
    return jax.shard_map(
        functools.partial(local, mesh.shape["grp"], mesh.shape["ang"]),
        mesh=mesh,
        in_specs=(
            P(None, ("grp", "ang"), None, None, None, None),
            P(("grp", "ang"), None),
            P(),
            P(),
            P(None, None, "ang"),
            P("grp", None),
            P("grp", None),
            P("grp"),
        ),
        out_specs=P(None, "grp", None, None, "ang"),
        check_vma=False,
    )
```

```python
import functools

import jax
import jax.numpy as jnp
from jax import lax
from jax.experimental import pallas as pl
from jax.experimental.pallas import tpu as pltpu
from jax.sharding import PartitionSpec as P

MESH = pl.DeviceIdType.MESH
F32, BF16 = jnp.float32, jnp.bfloat16
LANES, SUBS = 128, 8
UNROLL = 4

SIN_COEFFS = (0.999999996, -0.041666645, 0.000520815696, -3.09516959e-06, 1.01767836e-08)
COS_COEFFS = (0.999999953, -0.124999763, 0.00260397403, -2.1646421e-05, 9.04459312e-08)


def horner(coeffs, x):
    total = x * coeffs[-1] + coeffs[-2]
    for coeff in coeffs[-3::-1]:
        total = total * x + coeff
    return total


def sin_cos(angle):
    square = angle * angle
    twice_sine = angle * horner(SIN_COEFFS, square)
    return twice_sine * horner(COS_COEFFS, square), 1.0 - 0.5 * twice_sine * twice_sine


def iota(shape, axis):
    return lax.broadcasted_iota(jnp.int32, shape, axis)


def sublane_sums(rows, sub):
    low = (sub & 4) == 0
    rows = [
        jnp.where(low, rows[i], rows[i + 4]) + pltpu.roll(jnp.where(low, rows[i + 4], rows[i]), 4, 0)
        for i in range(4)
    ]
    for step in (2, 1):
        low = (sub & step) == 0
        rows = [
            jnp.where(low, rows[i], rows[i + step])
            + jnp.where(low, pltpu.roll(rows[i], SUBS - step, 0), pltpu.roll(rows[i + step], step, 0))
            for i in range(step)
        ]
    return rows[0]


def kernel(
    grp_size, ang_size, unroll,
    children_h, present_h, interp_h, phase_h, trans_h, sources_h, trans_ids_h, list_len_h,
    out,
    child_v, present, interp, phase, trans, sources, trans_ids, list_len, slabs, lhs,
    stage_a, stage_b, send, recv, picked, turned,
    load_sems, send_sem, recv_sems, forward_sems,
):
    my_grp, my_ang = lax.axis_index("grp"), lax.axis_index("ang")
    devices = grp_size * ang_size
    me = my_grp * ang_size + my_ang

    def wrap(index, size):
        return jnp.where(index >= size, index - size, index)

    def grp_at(step):
        return wrap(my_grp + step, grp_size)

    def ang_at(step):
        return wrap(my_ang + step, ang_size)

    pairs = (
        (children_h, child_v), (present_h, present), (interp_h, interp), (phase_h, phase),
        (trans_h, trans), (sources_h, sources), (trans_ids_h, trans_ids), (list_len_h, list_len),
    )
    loads = [pltpu.make_async_copy(src, dst, load_sems.at[i]) for i, (src, dst) in enumerate(pairs)]
    for load in loads:
        load.start()

    barrier = pltpu.get_barrier_semaphore()

    for step in range(1, ang_size):
        pl.semaphore_signal(barrier, inc=1, device_id=(my_grp, ang_at(step)), device_id_type=MESH)
    for step in range(1, grp_size):
        pl.semaphore_signal(barrier, inc=1, device_id=(grp_at(step), my_ang), device_id_type=MESH)

    loads[0].wait()
    loads[1].wait()
    sub = iota((SUBS, LANES), 0)
    octants = present.shape[1]
    mask = jnp.zeros((SUBS, LANES), F32)
    for octant in range(octants):
        mask = jnp.where(sub == octant, present[0, octant].astype(F32), mask)

    chunks = child_v.shape[0] // (2 * octants)
    chunk_tiles = child_v.shape[1] // 2
    coarse_tiles = chunks * chunk_tiles
    for row in range(child_v.shape[0]):
        slabs[row * 2 * chunk_tiles:(row + 1) * 2 * chunk_tiles, :] = child_v[row].astype(F32)
    half_width = interp.shape[0] // 2
    lane = iota((SUBS, LANES), 1)

    def shifted(here, before, by):
        return jnp.where(lane < by, pltpu.roll(before, by, 1), pltpu.roll(here, by, 1))

    for pol in range(2):
        groups = []
        for reim in range(2):
            tiles = [
                slabs[
                    pl.ds(
                        2 * chunk_tiles * (octants * chunks * reim + tile // chunk_tiles)
                        + 2 * (tile % chunk_tiles) + pol,
                        octants,
                        stride=2 * chunk_tiles * chunks,
                    ),
                    :,
                ] * mask
                for tile in range(coarse_tiles)
            ]
            groups.append(tiles)
        for tile in range(coarse_tiles):
            first = [shifted(g[tile], g[tile - 1], half_width) for g in groups]
            second = [
                shifted(g[(tile + 1) % coarse_tiles], g[tile], half_width + LANES // 2) for g in groups
            ]
            rows = slice(2 * octants * pol, 2 * octants * (pol + 1))
            lhs[tile, 0, rows, :] = jnp.concatenate(first, axis=0).astype(BF16)
            lhs[tile, 1, rows, :] = jnp.concatenate(second, axis=0).astype(BF16)

    loads[2].wait()
    loads[3].wait()

    band_rows = 48
    gap = iota((band_rows, LANES), 0) - iota((band_rows, LANES), 1) // 4
    band = jnp.where((gap >= 0) & (gap < SUBS), 1.0, 0.0).astype(BF16)
    turn = lane // 4

    def banded(weights):
        for step in (1, 2, 4):
            weights = jnp.where((turn & step) != 0, pltpu.roll(weights, step, 0), weights)
        high = weights.astype(BF16)
        low = (weights - high.astype(F32)).astype(BF16)
        return [jnp.concatenate([x] * (band_rows // SUBS), axis=0) * band for x in (high, low)]

    def blank(rows):
        return jnp.zeros((rows, LANES), BF16)

    def refine(block, stage):
        for half in range(2):
            x = lhs[block, half]
            cols = []
            for tile in range(2):
                at = pl.multiple_of((4 * block + 2 * half + tile) * LANES, LANES)
                pieces = []
                for piece in banded(interp[:, pl.ds(at, LANES)]):
                    pieces += [blank(32 * tile), piece] if tile else [piece]
                    pieces.append(blank(LANES - band_rows - 32 * tile))
                cols.append(jnp.concatenate(pieces, axis=0))
            stage[half] = jnp.dot(
                jnp.concatenate([x, x], axis=1), jnp.concatenate(cols, axis=1), preferred_element_type=F32
            )

    def combine(block, stage):
        real, imag = [], []
        for half in range(2):
            for tile in range(2):
                at = pl.multiple_of((4 * block + 2 * half + tile) * LANES, LANES)
                sine, cosine = sin_cos(phase[:, pl.ds(at, LANES)])
                cols = pl.ds(tile * LANES, LANES)
                for pol in range(2):
                    re = stage[half, 16 * pol:16 * pol + 8, cols]
                    im = stage[half, 16 * pol + 8:16 * pol + 16, cols]
                    real.append(re * cosine - im * sine)
                    imag.append(re * sine + im * cosine)
        send[block] = jnp.concatenate(
            [sublane_sums(real, sub), sublane_sums(imag, sub)], axis=0
        ).astype(BF16)

    def post(step, own):
        block = block_at(step)
        src, dst = send.at[block], recv.at[my_grp * ang_size + step]
        arrived = recv_sems.at[step // unroll]
        if own:
            pltpu.make_async_copy(src, dst, arrived).start()
        else:
            pltpu.make_async_remote_copy(
                src_ref=src, dst_ref=dst, send_sem=send_sem, recv_sem=arrived,
                device_id=(my_grp, block), device_id_type=MESH,
            ).start()

    def chunk_of(grp, group):
        return recv.at[pl.ds(grp * ang_size + group * unroll, unroll)]

    def forward(group):
        chunk = chunk_of(my_grp, group)
        pltpu.make_async_copy(chunk, chunk, recv_sems.at[group]).wait()
        for step in range(1, grp_size):
            pltpu.make_async_remote_copy(
                src_ref=chunk, dst_ref=chunk, send_sem=send_sem, recv_sem=forward_sems.at[step - 1, group],
                device_id=(grp_at(step), my_ang), device_id_type=MESH,
            ).start()

    def block_at(step):
        return ang_at(1 + step)

    def refine_group(group, stages):
        for i in range(unroll):
            refine(block_at(group * unroll + i), stages.at[i])

    def combine_group(group, stages):
        for i in range(unroll):
            combine(block_at(group * unroll + i), stages.at[i])

    def post_group(group, last=False):
        for i in range(unroll):
            post(group * unroll + i, last and i == unroll - 1)

    def one_round(step, last=False):
        refine_group(2 * step + 1, stage_b)
        combine_group(2 * step, stage_a)
        if isinstance(step, int) and step == 0:
            pl.semaphore_wait(barrier, ang_size + grp_size - 2)
        post_group(2 * step)
        if not (isinstance(step, int) and step == 0):
            forward(2 * step - 2)
        if not last:
            refine_group(2 * step + 2, stage_a)
        combine_group(2 * step + 1, stage_b)
        post_group(2 * step + 1, last)
        if not (isinstance(step, int) and step == 0):
            forward(2 * step - 1)

    def advance(step, carry):
        one_round(step)
        return carry

    refine_group(0, stage_a)
    rounds = ang_size // (2 * unroll)
    one_round(0, rounds == 1)
    if rounds > 2:
        lax.fori_loop(1, rounds - 1, advance, 0)
    if rounds > 1:
        one_round(rounds - 1, True)
    for group in range(2 * rounds - 2, 2 * rounds):
        forward(group)

    for load in loads[4:]:
        load.wait()
    slots, clusters = sources.shape
    even = (sub & 1) == 0

    def pick(cluster, carry):
        for slot in range(slots):
            source = sources[slot, cluster]
            source_grp = lax.div(source, ang_size)
            came = my_ang - 1 - (source - source_grp * ang_size)
            came = jnp.where(came < 0, came + ang_size, came)
            sources[slot, cluster] = source_grp * ang_size + came
            both = trans[trans_ids[slot, cluster]]
            both = both * jnp.where(slot < list_len[cluster], 1.0, 0.0)
            picked[cluster * slots + slot, 0] = jnp.where(even, both, pltpu.roll(both, 1, 0))
            picked[cluster * slots + slot, 1] = jnp.where(even, pltpu.roll(both, SUBS - 1, 0), both)
        return carry

    lax.fori_loop(0, clusters, pick, 0, unroll=2)

    for step in range(1, grp_size):
        for group in range(2 * rounds):
            chunk = chunk_of(wrap(my_grp + grp_size - step, grp_size), group)
            pltpu.make_async_copy(chunk, chunk, forward_sems.at[step - 1, group]).wait()

    def receive(cluster, carry):
        real = imag = jnp.zeros((SUBS, LANES), F32)
        for slot in range(slots):
            row = cluster * slots + slot
            op_re, op_im = picked[row, 0], picked[row, 1]
            both = recv[sources[slot, cluster]].astype(F32)
            src_re, src_im = both[0:SUBS], both[SUBS:2 * SUBS]
            real += op_re * src_re - op_im * src_im
            imag += op_re * src_im + op_im * src_re
        for part, value in enumerate((real, imag)):
            turned[cluster, part] = value
            for pol in range(2):
                out[part, cluster, 4 * pol:4 * pol + 4, :] = turned[cluster, part, pl.ds(pol, 4, stride=2), :]
        return carry

    lax.fori_loop(0, clusters, receive, 0, unroll=4)

    sent = recv.at[pl.ds(0, devices - 1)]
    pltpu.make_async_copy(sent, sent, send_sem).wait()


def local(grp_size, ang_size, children, present, interp, phase, trans, sources, trans_ids, list_len):
    parts, own, octants, pols, angles, coarse = children.shape
    operators, width = trans.shape[1:]
    clusters, slots = sources.shape
    assert ang_size % (2 * UNROLL) == 0
    devices = grp_size * ang_size
    quarters = width // LANES
    assert (parts, own, octants, pols, angles, quarters) == (2, 1, SUBS, 2, 1, 4)
    assert interp.shape[0] == SUBS and interp.shape[1] == ang_size * width == 4 * coarse
    chunk = SUBS * LANES
    children = children.reshape(parts * octants, pols, coarse // chunk, SUBS, LANES)
    children = children.transpose(0, 2, 3, 1, 4).reshape(parts * octants * coarse // chunk, 2 * SUBS, LANES)
    trans = trans.transpose(1, 0, 2).reshape(operators, parts, quarters, LANES)
    trans = trans.transpose(0, 2, 1, 3).reshape(operators, quarters * parts, LANES)
    operands = (children, present, interp, phase, trans, sources.T, trans_ids.T, list_len)
    tile_rows = 2 * SUBS
    operands = tuple(pltpu.with_memory_space_constraint(operand, pltpu.HBM) for operand in operands)
    received = pl.pallas_call(
        functools.partial(kernel, grp_size, ang_size, UNROLL),
        out_shape=jax.ShapeDtypeStruct((parts, clusters, SUBS, LANES), F32),
        in_specs=[pl.BlockSpec(memory_space=pltpu.HBM)] * len(operands),
        out_specs=pl.BlockSpec(memory_space=pltpu.VMEM),
        scratch_shapes=[
            *(
                (pltpu.SMEM if operand.dtype == jnp.int32 else pltpu.VMEM)(operand.shape, operand.dtype)
                for operand in operands
            ),
            pltpu.VMEM((children.size // LANES, LANES), F32),
            pltpu.VMEM((coarse // LANES, 2, parts * octants * pols, LANES), BF16),
            pltpu.VMEM((UNROLL, 2, parts * octants * pols, 2 * LANES), F32),
            pltpu.VMEM((UNROLL, 2, parts * octants * pols, 2 * LANES), F32),
            pltpu.VMEM((ang_size, tile_rows, LANES), BF16),
            pltpu.VMEM((devices, tile_rows, LANES), BF16),
            pltpu.VMEM((clusters * slots, 2, SUBS, LANES), F32),
            pltpu.VMEM((clusters, 2, SUBS, LANES), F32),
            pltpu.SemaphoreType.DMA((len(operands),)),
            pltpu.SemaphoreType.DMA,
            pltpu.SemaphoreType.DMA((ang_size // UNROLL,)),
            pltpu.SemaphoreType.DMA((max(grp_size - 1, 1), ang_size // UNROLL)),
        ],
        compiler_params=pltpu.CompilerParams(
            collective_id=0, has_side_effects=True, vmem_limit_bytes=48 * 1024 * 1024
        ),
    )(*operands)
    return received.reshape(parts, clusters, pols, angles, width)


def solution(mesh):
    return jax.shard_map(
        functools.partial(local, mesh.shape["grp"], mesh.shape["ang"]),
        mesh=mesh,
        in_specs=(
            P(None, ("grp", "ang"), None, None, None, None),
            P(("grp", "ang"), None),
            P(),
            P(),
            P(None, None, "ang"),
            P("grp", None),
            P("grp", None),
            P("grp"),
        ),
        out_specs=P(None, "grp", None, None, "ang"),
        check_vma=False,
    )
```

```python
import functools

import jax
import jax.numpy as jnp
from jax import lax
from jax.experimental import pallas as pl
from jax.experimental.pallas import tpu as pltpu
from jax.sharding import PartitionSpec as P

MESH = pl.DeviceIdType.MESH
F32, BF16 = jnp.float32, jnp.bfloat16
LANES, SUBS = 128, 8
UNROLL = 4

SIN_COEFFS = (0.999999996, -0.041666645, 0.000520815696, -3.09516959e-06, 1.01767836e-08)
COS_COEFFS = (0.999999953, -0.124999763, 0.00260397403, -2.1646421e-05, 9.04459312e-08)


def horner(coeffs, x):
    total = x * coeffs[-1] + coeffs[-2]
    for coeff in coeffs[-3::-1]:
        total = total * x + coeff
    return total


def sin_cos(angle):
    square = angle * angle
    twice_sine = angle * horner(SIN_COEFFS, square)
    return twice_sine * horner(COS_COEFFS, square), 1.0 - 0.5 * twice_sine * twice_sine


def iota(shape, axis):
    return lax.broadcasted_iota(jnp.int32, shape, axis)


def sublane_sums(rows, sub):
    low = (sub & 4) == 0
    rows = [
        jnp.where(low, rows[i], rows[i + 4]) + pltpu.roll(jnp.where(low, rows[i + 4], rows[i]), 4, 0)
        for i in range(4)
    ]
    for step in (2, 1):
        low = (sub & step) == 0
        rows = [
            jnp.where(low, rows[i], rows[i + step])
            + jnp.where(low, pltpu.roll(rows[i], SUBS - step, 0), pltpu.roll(rows[i + step], step, 0))
            for i in range(step)
        ]
    return rows[0]


def kernel(
    grp_size, ang_size, unroll,
    children_h, present_h, interp_h, phase_h, trans_h, sources_h, trans_ids_h, list_len_h,
    out,
    child_v, present, interp, phase, trans, sources, trans_ids, list_len, slabs, lhs,
    stage, send, recv, picked, turned,
    load_sems, send_sem, recv_sem,
):
    my_grp, my_ang = lax.axis_index("grp"), lax.axis_index("ang")
    devices = grp_size * ang_size
    me = my_grp * ang_size + my_ang

    def wrap(index, size):
        return jnp.where(index >= size, index - size, index)

    def grp_at(step):
        return wrap(my_grp + step, grp_size)

    def ang_at(step):
        return wrap(my_ang + step, ang_size)

    pairs = (
        (children_h, child_v), (present_h, present), (interp_h, interp), (phase_h, phase),
        (trans_h, trans), (sources_h, sources), (trans_ids_h, trans_ids), (list_len_h, list_len),
    )
    loads = [pltpu.make_async_copy(src, dst, load_sems.at[i]) for i, (src, dst) in enumerate(pairs)]
    for load in loads[:4]:
        load.start()

    barrier = pltpu.get_barrier_semaphore()

    for grp_step in range(grp_size):
        for ang_step in range(ang_size):
            if grp_step or ang_step:
                pl.semaphore_signal(
                    barrier, inc=1, device_id=(grp_at(grp_step), ang_at(ang_step)), device_id_type=MESH
                )

    loads[0].wait()
    loads[1].wait()
    sub = iota((SUBS, LANES), 0)
    octants = present.shape[1]
    mask = jnp.zeros((SUBS, LANES), F32)
    for octant in range(octants):
        mask = jnp.where(sub == octant, present[0, octant].astype(F32), mask)

    chunks = child_v.shape[0] // (2 * octants)
    chunk_tiles = child_v.shape[1] // 2
    coarse_tiles = chunks * chunk_tiles
    for row in range(child_v.shape[0]):
        slabs[row * 2 * chunk_tiles:(row + 1) * 2 * chunk_tiles, :] = child_v[row].astype(F32)
    half_width = interp.shape[0] // 2
    lane = iota((SUBS, LANES), 1)

    def shifted(here, before, by):
        return jnp.where(lane < by, pltpu.roll(before, by, 1), pltpu.roll(here, by, 1))

    for pol in range(2):
        groups = []
        for reim in range(2):
            tiles = [
                slabs[
                    pl.ds(
                        2 * chunk_tiles * (octants * chunks * reim + tile // chunk_tiles)
                        + 2 * (tile % chunk_tiles) + pol,
                        octants,
                        stride=2 * chunk_tiles * chunks,
                    ),
                    :,
                ] * mask
                for tile in range(coarse_tiles)
            ]
            groups.append(tiles)
        for tile in range(coarse_tiles):
            first = [shifted(g[tile], g[tile - 1], half_width) for g in groups]
            second = [
                shifted(g[(tile + 1) % coarse_tiles], g[tile], half_width + LANES // 2) for g in groups
            ]
            rows = slice(2 * octants * pol, 2 * octants * (pol + 1))
            lhs[tile, 0, rows, :] = jnp.concatenate(first, axis=0).astype(BF16)
            lhs[tile, 1, rows, :] = jnp.concatenate(second, axis=0).astype(BF16)

    loads[2].wait()
    loads[3].wait()
    for load in loads[4:]:
        load.start()

    band_rows = 48
    gap = iota((band_rows, LANES), 0) - iota((band_rows, LANES), 1) // 4
    band = jnp.where((gap >= 0) & (gap < SUBS), 1.0, 0.0).astype(BF16)
    turn = lane // 4

    def banded(weights):
        for step in (1, 2, 4):
            weights = jnp.where((turn & step) != 0, pltpu.roll(weights, step, 0), weights)
        high = weights.astype(BF16)
        low = (weights - high.astype(F32)).astype(BF16)
        return [jnp.concatenate([x] * (band_rows // SUBS), axis=0) * band for x in (high, low)]

    def blank(rows):
        return jnp.zeros((rows, LANES), BF16)

    def refine(block, stage):
        for half in range(2):
            x = lhs[block, half]
            cols = []
            for tile in range(2):
                at = pl.multiple_of((4 * block + 2 * half + tile) * LANES, LANES)
                pieces = []
                for piece in banded(interp[:, pl.ds(at, LANES)]):
                    pieces += [blank(32 * tile), piece] if tile else [piece]
                    pieces.append(blank(LANES - band_rows - 32 * tile))
                cols.append(jnp.concatenate(pieces, axis=0))
            stage[half] = jnp.dot(
                jnp.concatenate([x, x], axis=1), jnp.concatenate(cols, axis=1), preferred_element_type=F32
            )

    def combine(block, stage):
        real, imag = [], []
        for half in range(2):
            for tile in range(2):
                at = pl.multiple_of((4 * block + 2 * half + tile) * LANES, LANES)
                sine, cosine = sin_cos(phase[:, pl.ds(at, LANES)])
                cols = pl.ds(tile * LANES, LANES)
                for pol in range(2):
                    re = stage[half, 16 * pol:16 * pol + 8, cols]
                    im = stage[half, 16 * pol + 8:16 * pol + 16, cols]
                    real.append(re * cosine - im * sine)
                    imag.append(re * sine + im * cosine)
        send[block] = jnp.concatenate(
            [sublane_sums(real, sub), sublane_sums(imag, sub)], axis=0
        ).astype(BF16)

    def post(block, own):
        for step in range(grp_size):
            if own and not step:
                pltpu.make_async_copy(send.at[block], recv.at[me], recv_sem).start()
                continue
            pltpu.make_async_remote_copy(
                src_ref=send.at[block], dst_ref=recv.at[me], send_sem=send_sem, recv_sem=recv_sem,
                device_id=(grp_at(step), block), device_id_type=MESH,
            ).start()

    def block_at(step):
        return ang_at(1 + step)

    def refine_group(group, stages):
        for i in range(unroll):
            refine(block_at(group * unroll + i), stages.at[i])

    def combine_group(group, stages):
        for i in range(unroll):
            combine(block_at(group * unroll + i), stages.at[i])

    def post_group(group, last=False):
        for i in range(unroll):
            post(block_at(group * unroll + i), last and i == unroll - 1)

    def one_group(group, last=False):
        refine_group(group, stage)
        combine_group(group, stage)
        if isinstance(group, int) and group == 0:
            pl.semaphore_wait(barrier, devices - 1)
        post_group(group, last)

    def advance(group, carry):
        one_group(group)
        return carry

    groups = ang_size // unroll
    one_group(0, groups == 1)
    if groups > 2:
        lax.fori_loop(1, groups - 1, advance, 0)
    if groups > 1:
        one_group(groups - 1, True)

    for load in loads[4:]:
        load.wait()
    slots, clusters = sources.shape
    even = (sub & 1) == 0

    def pick(cluster, carry):
        for slot in range(slots):
            both = trans[trans_ids[slot, cluster]]
            both = both * jnp.where(slot < list_len[cluster], 1.0, 0.0)
            picked[cluster * slots + slot, 0] = jnp.where(even, both, pltpu.roll(both, 1, 0))
            picked[cluster * slots + slot, 1] = jnp.where(even, pltpu.roll(both, SUBS - 1, 0), both)
        return carry

    lax.fori_loop(0, clusters, pick, 0, unroll=2)

    pltpu.make_async_copy(recv, recv, recv_sem).wait()

    def receive(cluster, carry):
        real = imag = jnp.zeros((SUBS, LANES), F32)
        for slot in range(slots):
            source = sources[slot, cluster]
            row = cluster * slots + slot
            op_re, op_im = picked[row, 0], picked[row, 1]
            both = recv[source].astype(F32)
            src_re, src_im = both[0:SUBS], both[SUBS:2 * SUBS]
            real += op_re * src_re - op_im * src_im
            imag += op_re * src_im + op_im * src_re
        for part, value in enumerate((real, imag)):
            turned[cluster, part] = value
            for pol in range(2):
                out[part, cluster, 4 * pol:4 * pol + 4, :] = turned[cluster, part, pl.ds(pol, 4, stride=2), :]
        return carry

    lax.fori_loop(0, clusters, receive, 0, unroll=4)

    sent = recv.at[pl.ds(0, devices - 1)]
    pltpu.make_async_copy(sent, sent, send_sem).wait()


def local(grp_size, ang_size, children, present, interp, phase, trans, sources, trans_ids, list_len):
    parts, own, octants, pols, angles, coarse = children.shape
    operators, width = trans.shape[1:]
    clusters, slots = sources.shape
    assert ang_size % UNROLL == 0
    devices = grp_size * ang_size
    quarters = width // LANES
    assert (parts, own, octants, pols, angles, quarters) == (2, 1, SUBS, 2, 1, 4)
    assert interp.shape[0] == SUBS and interp.shape[1] == ang_size * width == 4 * coarse
    chunk = SUBS * LANES
    children = children.reshape(parts * octants, pols, coarse // chunk, SUBS, LANES)
    children = children.transpose(0, 2, 3, 1, 4).reshape(parts * octants * coarse // chunk, 2 * SUBS, LANES)
    trans = trans.transpose(1, 0, 2).reshape(operators, parts, quarters, LANES)
    trans = trans.transpose(0, 2, 1, 3).reshape(operators, quarters * parts, LANES)
    operands = (children, present, interp, phase, trans, sources.T, trans_ids.T, list_len)
    tile_rows = 2 * SUBS
    operands = tuple(pltpu.with_memory_space_constraint(operand, pltpu.HBM) for operand in operands)
    received = pl.pallas_call(
        functools.partial(kernel, grp_size, ang_size, UNROLL),
        out_shape=jax.ShapeDtypeStruct((parts, clusters, SUBS, LANES), F32),
        in_specs=[pl.BlockSpec(memory_space=pltpu.HBM)] * len(operands),
        out_specs=pl.BlockSpec(memory_space=pltpu.VMEM),
        scratch_shapes=[
            *(
                (pltpu.SMEM if operand.dtype == jnp.int32 else pltpu.VMEM)(operand.shape, operand.dtype)
                for operand in operands
            ),
            pltpu.VMEM((children.size // LANES, LANES), F32),
            pltpu.VMEM((coarse // LANES, 2, parts * octants * pols, LANES), BF16),
            pltpu.VMEM((UNROLL, 2, parts * octants * pols, 2 * LANES), F32),
            pltpu.VMEM((ang_size, tile_rows, LANES), BF16),
            pltpu.VMEM((devices, tile_rows, LANES), BF16),
            pltpu.VMEM((clusters * slots, 2, SUBS, LANES), F32),
            pltpu.VMEM((clusters, 2, SUBS, LANES), F32),
            pltpu.SemaphoreType.DMA((len(operands),)),
            pltpu.SemaphoreType.DMA,
            pltpu.SemaphoreType.DMA,
        ],
        compiler_params=pltpu.CompilerParams(
            collective_id=0, has_side_effects=True, vmem_limit_bytes=48 * 1024 * 1024
        ),
    )(*operands)
    return received.reshape(parts, clusters, pols, angles, width)


def solution(mesh):
    return jax.shard_map(
        functools.partial(local, mesh.shape["grp"], mesh.shape["ang"]),
        mesh=mesh,
        in_specs=(
            P(None, ("grp", "ang"), None, None, None, None),
            P(("grp", "ang"), None),
            P(),
            P(),
            P(None, None, "ang"),
            P("grp", None),
            P("grp", None),
            P("grp"),
        ),
        out_specs=P(None, "grp", None, None, "ang"),
        check_vma=False,
    )
```

```python
import functools

import jax
import jax.numpy as jnp
from jax import lax
from jax.experimental import pallas as pl
from jax.experimental.pallas import tpu as pltpu
from jax.sharding import PartitionSpec as P

MESH = pl.DeviceIdType.MESH
F32, BF16 = jnp.float32, jnp.bfloat16
LANES, SUBS = 128, 8
UNROLL = 4

SIN_COEFFS = (0.999999996, -0.041666645, 0.000520815696, -3.09516959e-06, 1.01767836e-08)
COS_COEFFS = (0.999999953, -0.124999763, 0.00260397403, -2.1646421e-05, 9.04459312e-08)


def horner(coeffs, x):
    total = x * coeffs[-1] + coeffs[-2]
    for coeff in coeffs[-3::-1]:
        total = total * x + coeff
    return total


def sin_cos(angle):
    square = angle * angle
    twice_sine = angle * horner(SIN_COEFFS, square)
    return twice_sine * horner(COS_COEFFS, square), 1.0 - 0.5 * twice_sine * twice_sine


def iota(shape, axis):
    return lax.broadcasted_iota(jnp.int32, shape, axis)


def sublane_sums(rows, sub):
    low = (sub & 4) == 0
    rows = [
        jnp.where(low, rows[i], rows[i + 4]) + pltpu.roll(jnp.where(low, rows[i + 4], rows[i]), 4, 0)
        for i in range(4)
    ]
    for step in (2, 1):
        low = (sub & step) == 0
        rows = [
            jnp.where(low, rows[i], rows[i + step])
            + jnp.where(low, pltpu.roll(rows[i], SUBS - step, 0), pltpu.roll(rows[i + step], step, 0))
            for i in range(step)
        ]
    return rows[0]


def kernel(
    grp_size, ang_size, unroll,
    children_h, present_h, interp_h, phase_h, trans_h, sources_h, trans_ids_h, list_len_h,
    out,
    child_v, present, interp, phase, trans, sources, trans_ids, list_len, slabs, lhs,
    stage, send, recv, picked, turned,
    load_sems, send_sem, recv_sem,
):
    my_grp, my_ang = lax.axis_index("grp"), lax.axis_index("ang")
    devices = grp_size * ang_size
    me = my_grp * ang_size + my_ang

    def wrap(index, size):
        return jnp.where(index >= size, index - size, index)

    def grp_at(step):
        return wrap(my_grp + step, grp_size)

    def ang_at(step):
        return wrap(my_ang + step, ang_size)

    pairs = (
        (children_h, child_v), (present_h, present), (interp_h, interp), (phase_h, phase),
        (trans_h, trans), (sources_h, sources), (trans_ids_h, trans_ids), (list_len_h, list_len),
    )
    loads = [pltpu.make_async_copy(src, dst, load_sems.at[i]) for i, (src, dst) in enumerate(pairs)]
    for load in loads[:4]:
        load.start()

    barrier = pltpu.get_barrier_semaphore()

    def greet(ang_step, carry):
        for grp_step in range(grp_size):
            pl.semaphore_signal(
                barrier, inc=1, device_id=(grp_at(grp_step), ang_at(ang_step)), device_id_type=MESH
            )
        return carry

    lax.fori_loop(1, ang_size, greet, 0)
    for grp_step in range(1, grp_size):
        pl.semaphore_signal(barrier, inc=1, device_id=(grp_at(grp_step), my_ang), device_id_type=MESH)

    loads[0].wait()
    loads[1].wait()
    sub = iota((SUBS, LANES), 0)
    octants = present.shape[1]
    mask = jnp.zeros((SUBS, LANES), F32)
    for octant in range(octants):
        mask = jnp.where(sub == octant, present[0, octant].astype(F32), mask)

    chunks = child_v.shape[0] // (2 * octants)
    chunk_tiles = child_v.shape[1] // 2
    coarse_tiles = chunks * chunk_tiles
    for row in range(child_v.shape[0]):
        slabs[row * 2 * chunk_tiles:(row + 1) * 2 * chunk_tiles, :] = child_v[row].astype(F32)
    half_width = interp.shape[0] // 2
    lane = iota((SUBS, LANES), 1)

    def shifted(here, before, by):
        return jnp.where(lane < by, pltpu.roll(before, by, 1), pltpu.roll(here, by, 1))

    for pol in range(2):
        groups = []
        for reim in range(2):
            tiles = [
                slabs[
                    pl.ds(
                        2 * chunk_tiles * (octants * chunks * reim + tile // chunk_tiles)
                        + 2 * (tile % chunk_tiles) + pol,
                        octants,
                        stride=2 * chunk_tiles * chunks,
                    ),
                    :,
                ] * mask
                for tile in range(coarse_tiles)
            ]
            groups.append(tiles)
        for tile in range(coarse_tiles):
            first = [shifted(g[tile], g[tile - 1], half_width) for g in groups]
            second = [
                shifted(g[(tile + 1) % coarse_tiles], g[tile], half_width + LANES // 2) for g in groups
            ]
            rows = slice(2 * octants * pol, 2 * octants * (pol + 1))
            lhs[tile, 0, rows, :] = jnp.concatenate(first, axis=0).astype(BF16)
            lhs[tile, 1, rows, :] = jnp.concatenate(second, axis=0).astype(BF16)

    loads[2].wait()
    loads[3].wait()
    for load in loads[4:]:
        load.start()

    band_rows = 48
    gap = iota((band_rows, LANES), 0) - iota((band_rows, LANES), 1) // 4
    band = jnp.where((gap >= 0) & (gap < SUBS), 1.0, 0.0).astype(BF16)
    turn = lane // 4

    def banded(weights):
        for step in (1, 2, 4):
            weights = jnp.where((turn & step) != 0, pltpu.roll(weights, step, 0), weights)
        high = weights.astype(BF16)
        low = (weights - high.astype(F32)).astype(BF16)
        return [jnp.concatenate([x] * (band_rows // SUBS), axis=0) * band for x in (high, low)]

    def blank(rows):
        return jnp.zeros((rows, LANES), BF16)

    def refine(block, stage):
        for half in range(2):
            x = lhs[block, half]
            cols = []
            for tile in range(2):
                at = pl.multiple_of((4 * block + 2 * half + tile) * LANES, LANES)
                pieces = []
                for piece in banded(interp[:, pl.ds(at, LANES)]):
                    pieces += [blank(32 * tile), piece] if tile else [piece]
                    pieces.append(blank(LANES - band_rows - 32 * tile))
                cols.append(jnp.concatenate(pieces, axis=0))
            stage[half] = jnp.dot(
                jnp.concatenate([x, x], axis=1), jnp.concatenate(cols, axis=1), preferred_element_type=F32
            )

    def combine(block, stage):
        real, imag = [], []
        for half in range(2):
            for tile in range(2):
                at = pl.multiple_of((4 * block + 2 * half + tile) * LANES, LANES)
                sine, cosine = sin_cos(phase[:, pl.ds(at, LANES)])
                cols = pl.ds(tile * LANES, LANES)
                for pol in range(2):
                    re = stage[half, 16 * pol:16 * pol + 8, cols]
                    im = stage[half, 16 * pol + 8:16 * pol + 16, cols]
                    real.append(re * cosine - im * sine)
                    imag.append(re * sine + im * cosine)
        send[block] = jnp.concatenate(
            [sublane_sums(real, sub), sublane_sums(imag, sub)], axis=0
        ).astype(BF16)

    def post(block, may_be_own):
        for step in range(grp_size):

            def away():
                pltpu.make_async_remote_copy(
                    src_ref=send.at[block], dst_ref=recv.at[me], send_sem=send_sem, recv_sem=recv_sem,
                    device_id=(grp_at(step), block), device_id_type=MESH,
                ).start()

            if step or not may_be_own:
                away()
            else:
                pl.when(block != my_ang)(away)

                @pl.when(block == my_ang)
                def _():
                    pltpu.make_async_copy(send.at[block], recv.at[me], recv_sem).start()

    def block_at(step):
        return ang_at(1 + step)

    def refine_group(group, stages):
        for i in range(unroll):
            refine(block_at(group * unroll + i), stages.at[i])

    def combine_group(group, stages):
        for i in range(unroll):
            combine(block_at(group * unroll + i), stages.at[i])

    def post_group(group):
        for i in range(unroll):
            post(block_at(group * unroll + i), i == unroll - 1)

    def one_group(group, carry):
        refine_group(group, stage)
        combine_group(group, stage)

        @pl.when(group == 0)
        def _():
            pl.semaphore_wait(barrier, devices - 1)

        post_group(group)
        return carry

    lax.fori_loop(0, ang_size // unroll, one_group, 0)

    for load in loads[4:]:
        load.wait()
    slots, clusters = sources.shape
    even = (sub & 1) == 0

    def pick(cluster, carry):
        for slot in range(slots):
            both = trans[trans_ids[slot, cluster]]
            both = both * jnp.where(slot < list_len[cluster], 1.0, 0.0)
            picked[cluster * slots + slot, 0] = jnp.where(even, both, pltpu.roll(both, 1, 0))
            picked[cluster * slots + slot, 1] = jnp.where(even, pltpu.roll(both, SUBS - 1, 0), both)
        return carry

    lax.fori_loop(0, clusters, pick, 0, unroll=2)

    pltpu.make_async_copy(recv, recv, recv_sem).wait()

    def receive(cluster, carry):
        real = imag = jnp.zeros((SUBS, LANES), F32)
        for slot in range(slots):
            source = sources[slot, cluster]
            row = cluster * slots + slot
            op_re, op_im = picked[row, 0], picked[row, 1]
            both = recv[source].astype(F32)
            src_re, src_im = both[0:SUBS], both[SUBS:2 * SUBS]
            real += op_re * src_re - op_im * src_im
            imag += op_re * src_im + op_im * src_re
        for part, value in enumerate((real, imag)):
            turned[cluster, part] = value
            for pol in range(2):
                out[part, cluster, 4 * pol:4 * pol + 4, :] = turned[cluster, part, pl.ds(pol, 4, stride=2), :]
        return carry

    lax.fori_loop(0, clusters, receive, 0, unroll=4)

    sent = recv.at[pl.ds(0, devices - 1)]
    pltpu.make_async_copy(sent, sent, send_sem).wait()


def local(grp_size, ang_size, children, present, interp, phase, trans, sources, trans_ids, list_len):
    parts, own, octants, pols, angles, coarse = children.shape
    operators, width = trans.shape[1:]
    clusters, slots = sources.shape
    assert ang_size % UNROLL == 0
    devices = grp_size * ang_size
    quarters = width // LANES
    assert (parts, own, octants, pols, angles, quarters) == (2, 1, SUBS, 2, 1, 4)
    assert interp.shape[0] == SUBS and interp.shape[1] == ang_size * width == 4 * coarse
    chunk = SUBS * LANES
    children = children.reshape(parts * octants, pols, coarse // chunk, SUBS, LANES)
    children = children.transpose(0, 2, 3, 1, 4).reshape(parts * octants * coarse // chunk, 2 * SUBS, LANES)
    trans = trans.transpose(1, 0, 2).reshape(operators, parts, quarters, LANES)
    trans = trans.transpose(0, 2, 1, 3).reshape(operators, quarters * parts, LANES)
    operands = (children, present, interp, phase, trans, sources.T, trans_ids.T, list_len)
    tile_rows = 2 * SUBS
    operands = tuple(pltpu.with_memory_space_constraint(operand, pltpu.HBM) for operand in operands)
    received = pl.pallas_call(
        functools.partial(kernel, grp_size, ang_size, UNROLL),
        out_shape=jax.ShapeDtypeStruct((parts, clusters, SUBS, LANES), F32),
        in_specs=[pl.BlockSpec(memory_space=pltpu.HBM)] * len(operands),
        out_specs=pl.BlockSpec(memory_space=pltpu.VMEM),
        scratch_shapes=[
            *(
                (pltpu.SMEM if operand.dtype == jnp.int32 else pltpu.VMEM)(operand.shape, operand.dtype)
                for operand in operands
            ),
            pltpu.VMEM((children.size // LANES, LANES), F32),
            pltpu.VMEM((coarse // LANES, 2, parts * octants * pols, LANES), BF16),
            pltpu.VMEM((UNROLL, 2, parts * octants * pols, 2 * LANES), F32),
            pltpu.VMEM((ang_size, tile_rows, LANES), BF16),
            pltpu.VMEM((devices, tile_rows, LANES), BF16),
            pltpu.VMEM((clusters * slots, 2, SUBS, LANES), F32),
            pltpu.VMEM((clusters, 2, SUBS, LANES), F32),
            pltpu.SemaphoreType.DMA((len(operands),)),
            pltpu.SemaphoreType.DMA,
            pltpu.SemaphoreType.DMA,
        ],
        compiler_params=pltpu.CompilerParams(
            collective_id=0, has_side_effects=True, vmem_limit_bytes=48 * 1024 * 1024
        ),
    )(*operands)
    return received.reshape(parts, clusters, pols, angles, width)


def solution(mesh):
    return jax.shard_map(
        functools.partial(local, mesh.shape["grp"], mesh.shape["ang"]),
        mesh=mesh,
        in_specs=(
            P(None, ("grp", "ang"), None, None, None, None),
            P(("grp", "ang"), None),
            P(),
            P(),
            P(None, None, "ang"),
            P("grp", None),
            P("grp", None),
            P("grp"),
        ),
        out_specs=P(None, "grp", None, None, "ang"),
        check_vma=False,
    )
```

```python
import functools

import jax
import jax.numpy as jnp
from jax import lax
from jax.experimental import pallas as pl
from jax.experimental.pallas import tpu as pltpu
from jax.sharding import PartitionSpec as P

MESH = pl.DeviceIdType.MESH
F32, BF16 = jnp.float32, jnp.bfloat16
LANES, SUBS = 128, 8
UNROLL = 4

SIN_COEFFS = (0.999999996, -0.041666645, 0.000520815696, -3.09516959e-06, 1.01767836e-08)
COS_COEFFS = (0.999999953, -0.124999763, 0.00260397403, -2.1646421e-05, 9.04459312e-08)


def horner(coeffs, x):
    total = x * coeffs[-1] + coeffs[-2]
    for coeff in coeffs[-3::-1]:
        total = total * x + coeff
    return total


def sin_cos(angle):
    square = angle * angle
    twice_sine = angle * horner(SIN_COEFFS, square)
    return twice_sine * horner(COS_COEFFS, square), 1.0 - 0.5 * twice_sine * twice_sine


def iota(shape, axis):
    return lax.broadcasted_iota(jnp.int32, shape, axis)


def sublane_sums(rows, sub):
    low = (sub & 4) == 0
    rows = [
        jnp.where(low, rows[i], rows[i + 4]) + pltpu.roll(jnp.where(low, rows[i + 4], rows[i]), 4, 0)
        for i in range(4)
    ]
    for step in (2, 1):
        low = (sub & step) == 0
        rows = [
            jnp.where(low, rows[i], rows[i + step])
            + jnp.where(low, pltpu.roll(rows[i], SUBS - step, 0), pltpu.roll(rows[i + step], step, 0))
            for i in range(step)
        ]
    return rows[0]


def kernel(
    grp_size, ang_size, unroll,
    children_h, present_h, interp_h, phase_h, trans_h, sources_h, trans_ids_h, list_len_h,
    out,
    child_v, present, interp, phase, trans, sources, trans_ids, list_len, slabs, lhs,
    stage, send, recv, picked, turned,
    load_sems, send_sem, recv_sem,
):
    my_grp, my_ang = lax.axis_index("grp"), lax.axis_index("ang")
    devices = grp_size * ang_size
    me = my_grp * ang_size + my_ang

    def wrap(index, size):
        return jnp.where(index >= size, index - size, index)

    def grp_at(step):
        return wrap(my_grp + step, grp_size)

    def ang_at(step):
        return wrap(my_ang + step, ang_size)

    pairs = (
        (children_h, child_v), (present_h, present), (interp_h, interp), (phase_h, phase),
        (trans_h, trans), (sources_h, sources), (trans_ids_h, trans_ids), (list_len_h, list_len),
    )
    loads = [pltpu.make_async_copy(src, dst, load_sems.at[i]) for i, (src, dst) in enumerate(pairs)]
    for load in loads[:4]:
        load.start()

    barrier = pltpu.get_barrier_semaphore()

    def greet(ang_step, carry):
        for grp_step in range(grp_size):
            pl.semaphore_signal(
                barrier, inc=1, device_id=(grp_at(grp_step), ang_at(ang_step)), device_id_type=MESH
            )
        return carry

    lax.fori_loop(1, ang_size, greet, 0)
    for grp_step in range(1, grp_size):
        pl.semaphore_signal(barrier, inc=1, device_id=(grp_at(grp_step), my_ang), device_id_type=MESH)

    loads[0].wait()
    loads[1].wait()
    sub = iota((SUBS, LANES), 0)
    octants = present.shape[1]
    mask = jnp.zeros((SUBS, LANES), F32)
    for octant in range(octants):
        mask = jnp.where(sub == octant, present[0, octant].astype(F32), mask)

    chunks = child_v.shape[0] // (2 * octants)
    chunk_tiles = child_v.shape[1] // 2
    coarse_tiles = chunks * chunk_tiles
    for row in range(child_v.shape[0]):
        slabs[row * 2 * chunk_tiles:(row + 1) * 2 * chunk_tiles, :] = child_v[row].astype(F32)
    half_width = interp.shape[0] // 2
    lane = iota((SUBS, LANES), 1)

    def shifted(here, before, by):
        return jnp.where(lane < by, pltpu.roll(before, by, 1), pltpu.roll(here, by, 1))

    for pol in range(2):
        groups = []
        for reim in range(2):
            tiles = [
                slabs[
                    pl.ds(
                        2 * chunk_tiles * (octants * chunks * reim + tile // chunk_tiles)
                        + 2 * (tile % chunk_tiles) + pol,
                        octants,
                        stride=2 * chunk_tiles * chunks,
                    ),
                    :,
                ] * mask
                for tile in range(coarse_tiles)
            ]
            groups.append(tiles)
        for tile in range(coarse_tiles):
            first = [shifted(g[tile], g[tile - 1], half_width) for g in groups]
            second = [
                shifted(g[(tile + 1) % coarse_tiles], g[tile], half_width + LANES // 2) for g in groups
            ]
            rows = slice(2 * octants * pol, 2 * octants * (pol + 1))
            lhs[tile, 0, rows, :] = jnp.concatenate(first, axis=0).astype(BF16)
            lhs[tile, 1, rows, :] = jnp.concatenate(second, axis=0).astype(BF16)

    loads[2].wait()
    loads[3].wait()
    for load in loads[4:]:
        load.start()

    band_rows = 48
    gap = iota((band_rows, LANES), 0) - iota((band_rows, LANES), 1) // 4
    band = jnp.where((gap >= 0) & (gap < SUBS), 1.0, 0.0).astype(BF16)
    turn = lane // 4

    def banded(weights):
        for step in (1, 2, 4):
            weights = jnp.where((turn & step) != 0, pltpu.roll(weights, step, 0), weights)
        high = weights.astype(BF16)
        low = (weights - high.astype(F32)).astype(BF16)
        return [jnp.concatenate([x] * (band_rows // SUBS), axis=0) * band for x in (high, low)]

    def blank(rows):
        return jnp.zeros((rows, LANES), BF16)

    def refine(block, stage):
        for half in range(2):
            x = lhs[block, half]
            cols = []
            for tile in range(2):
                at = pl.multiple_of((4 * block + 2 * half + tile) * LANES, LANES)
                pieces = []
                for piece in banded(interp[:, pl.ds(at, LANES)]):
                    pieces += [blank(32 * tile), piece] if tile else [piece]
                    pieces.append(blank(LANES - band_rows - 32 * tile))
                cols.append(jnp.concatenate(pieces, axis=0))
            stage[half] = jnp.dot(
                jnp.concatenate([x, x], axis=1), jnp.concatenate(cols, axis=1), preferred_element_type=F32
            )

    def combine(block, stage):
        real, imag = [], []
        for half in range(2):
            for tile in range(2):
                at = pl.multiple_of((4 * block + 2 * half + tile) * LANES, LANES)
                sine, cosine = sin_cos(phase[:, pl.ds(at, LANES)])
                cols = pl.ds(tile * LANES, LANES)
                for pol in range(2):
                    re = stage[half, 16 * pol:16 * pol + 8, cols]
                    im = stage[half, 16 * pol + 8:16 * pol + 16, cols]
                    real.append(re * cosine - im * sine)
                    imag.append(re * sine + im * cosine)
        send[block] = jnp.concatenate(
            [sublane_sums(real, sub), sublane_sums(imag, sub)], axis=0
        ).astype(BF16)

    def post(block, own):
        for step in range(grp_size):
            if own and not step:
                pltpu.make_async_copy(send.at[block], recv.at[me], recv_sem).start()
                continue
            pltpu.make_async_remote_copy(
                src_ref=send.at[block], dst_ref=recv.at[me], send_sem=send_sem, recv_sem=recv_sem,
                device_id=(grp_at(step), block), device_id_type=MESH,
            ).start()

    def block_at(step):
        return ang_at(1 + step)

    def refine_group(group, stages):
        for i in range(unroll):
            refine(block_at(group * unroll + i), stages.at[i])

    def combine_group(group, stages):
        for i in range(unroll):
            combine(block_at(group * unroll + i), stages.at[i])

    def one_group(group, carry):
        refine_group(group, stage)
        combine_group(group, stage)
        return carry

    lax.fori_loop(0, ang_size // unroll, one_group, 0)
    pl.semaphore_wait(barrier, devices - 1)

    def post_step(step, carry):
        post(block_at(step), False)
        return carry

    lax.fori_loop(0, ang_size - 1, post_step, 0, unroll=5 if ang_size % 5 == 1 else 1)
    post(my_ang, True)

    for load in loads[4:]:
        load.wait()
    slots, clusters = sources.shape
    even = (sub & 1) == 0

    def pick(cluster, carry):
        for slot in range(slots):
            both = trans[trans_ids[slot, cluster]]
            both = both * jnp.where(slot < list_len[cluster], 1.0, 0.0)
            picked[cluster * slots + slot, 0] = jnp.where(even, both, pltpu.roll(both, 1, 0))
            picked[cluster * slots + slot, 1] = jnp.where(even, pltpu.roll(both, SUBS - 1, 0), both)
        return carry

    lax.fori_loop(0, clusters, pick, 0, unroll=2)

    pltpu.make_async_copy(recv, recv, recv_sem).wait()

    def receive(cluster, carry):
        real = imag = jnp.zeros((SUBS, LANES), F32)
        for slot in range(slots):
            source = sources[slot, cluster]
            row = cluster * slots + slot
            op_re, op_im = picked[row, 0], picked[row, 1]
            both = recv[source].astype(F32)
            src_re, src_im = both[0:SUBS], both[SUBS:2 * SUBS]
            real += op_re * src_re - op_im * src_im
            imag += op_re * src_im + op_im * src_re
        for part, value in enumerate((real, imag)):
            turned[cluster, part] = value
            for pol in range(2):
                out[part, cluster, 4 * pol:4 * pol + 4, :] = turned[cluster, part, pl.ds(pol, 4, stride=2), :]
        return carry

    lax.fori_loop(0, clusters, receive, 0, unroll=4)

    sent = recv.at[pl.ds(0, devices - 1)]
    pltpu.make_async_copy(sent, sent, send_sem).wait()


def local(grp_size, ang_size, children, present, interp, phase, trans, sources, trans_ids, list_len):
    parts, own, octants, pols, angles, coarse = children.shape
    operators, width = trans.shape[1:]
    clusters, slots = sources.shape
    assert ang_size % UNROLL == 0
    devices = grp_size * ang_size
    quarters = width // LANES
    assert (parts, own, octants, pols, angles, quarters) == (2, 1, SUBS, 2, 1, 4)
    assert interp.shape[0] == SUBS and interp.shape[1] == ang_size * width == 4 * coarse
    chunk = SUBS * LANES
    children = children.reshape(parts * octants, pols, coarse // chunk, SUBS, LANES)
    children = children.transpose(0, 2, 3, 1, 4).reshape(parts * octants * coarse // chunk, 2 * SUBS, LANES)
    trans = trans.transpose(1, 0, 2).reshape(operators, parts, quarters, LANES)
    trans = trans.transpose(0, 2, 1, 3).reshape(operators, quarters * parts, LANES)
    operands = (children, present, interp, phase, trans, sources.T, trans_ids.T, list_len)
    tile_rows = 2 * SUBS
    operands = tuple(pltpu.with_memory_space_constraint(operand, pltpu.HBM) for operand in operands)
    received = pl.pallas_call(
        functools.partial(kernel, grp_size, ang_size, UNROLL),
        out_shape=jax.ShapeDtypeStruct((parts, clusters, SUBS, LANES), F32),
        in_specs=[pl.BlockSpec(memory_space=pltpu.HBM)] * len(operands),
        out_specs=pl.BlockSpec(memory_space=pltpu.VMEM),
        scratch_shapes=[
            *(
                (pltpu.SMEM if operand.dtype == jnp.int32 else pltpu.VMEM)(operand.shape, operand.dtype)
                for operand in operands
            ),
            pltpu.VMEM((children.size // LANES, LANES), F32),
            pltpu.VMEM((coarse // LANES, 2, parts * octants * pols, LANES), BF16),
            pltpu.VMEM((UNROLL, 2, parts * octants * pols, 2 * LANES), F32),
            pltpu.VMEM((ang_size, tile_rows, LANES), BF16),
            pltpu.VMEM((devices, tile_rows, LANES), BF16),
            pltpu.VMEM((clusters * slots, 2, SUBS, LANES), F32),
            pltpu.VMEM((clusters, 2, SUBS, LANES), F32),
            pltpu.SemaphoreType.DMA((len(operands),)),
            pltpu.SemaphoreType.DMA,
            pltpu.SemaphoreType.DMA,
        ],
        compiler_params=pltpu.CompilerParams(
            collective_id=0, has_side_effects=True, vmem_limit_bytes=48 * 1024 * 1024
        ),
    )(*operands)
    return received.reshape(parts, clusters, pols, angles, width)


def solution(mesh):
    return jax.shard_map(
        functools.partial(local, mesh.shape["grp"], mesh.shape["ang"]),
        mesh=mesh,
        in_specs=(
            P(None, ("grp", "ang"), None, None, None, None),
            P(("grp", "ang"), None),
            P(),
            P(),
            P(None, None, "ang"),
            P("grp", None),
            P("grp", None),
            P("grp"),
        ),
        out_specs=P(None, "grp", None, None, "ang"),
        check_vma=False,
    )
```

```python
import functools

import jax
import jax.numpy as jnp
from jax import lax
from jax.experimental import pallas as pl
from jax.experimental.pallas import tpu as pltpu
from jax.sharding import PartitionSpec as P

MESH = pl.DeviceIdType.MESH
F32, BF16 = jnp.float32, jnp.bfloat16
LANES, SUBS = 128, 8
UNROLL = 4

SIN_COEFFS = (0.999999996, -0.041666645, 0.000520815696, -3.09516959e-06, 1.01767836e-08)
COS_COEFFS = (0.999999953, -0.124999763, 0.00260397403, -2.1646421e-05, 9.04459312e-08)


def horner(coeffs, x):
    total = x * coeffs[-1] + coeffs[-2]
    for coeff in coeffs[-3::-1]:
        total = total * x + coeff
    return total


def sin_cos(angle):
    square = angle * angle
    twice_sine = angle * horner(SIN_COEFFS, square)
    return twice_sine * horner(COS_COEFFS, square), 1.0 - 0.5 * twice_sine * twice_sine


def iota(shape, axis):
    return lax.broadcasted_iota(jnp.int32, shape, axis)


def sublane_sums(rows, sub):
    low = (sub & 4) == 0
    rows = [
        jnp.where(low, rows[i], rows[i + 4]) + pltpu.roll(jnp.where(low, rows[i + 4], rows[i]), 4, 0)
        for i in range(4)
    ]
    for step in (2, 1):
        low = (sub & step) == 0
        rows = [
            jnp.where(low, rows[i], rows[i + step])
            + jnp.where(low, pltpu.roll(rows[i], SUBS - step, 0), pltpu.roll(rows[i + step], step, 0))
            for i in range(step)
        ]
    return rows[0]


def kernel(
    grp_size, ang_size, unroll,
    children_h, present_h, interp_h, phase_h, trans_h, sources_h, trans_ids_h, list_len_h,
    out,
    child_v, present, interp, phase, trans, sources, trans_ids, list_len, slabs, lhs,
    stage_a, stage_b, send, recv, picked, turned,
    load_sems, send_sem, recv_sem,
):
    my_grp, my_ang = lax.axis_index("grp"), lax.axis_index("ang")
    devices = grp_size * ang_size
    me = my_grp * ang_size + my_ang

    def wrap(index, size):
        return jnp.where(index >= size, index - size, index)

    def grp_at(step):
        return wrap(my_grp + step, grp_size)

    def ang_at(step):
        return wrap(my_ang + step, ang_size)

    pairs = (
        (children_h, child_v), (present_h, present), (interp_h, interp), (phase_h, phase),
        (trans_h, trans), (sources_h, sources), (trans_ids_h, trans_ids), (list_len_h, list_len),
    )
    loads = [pltpu.make_async_copy(src, dst, load_sems.at[i]) for i, (src, dst) in enumerate(pairs)]
    for load in loads[:4]:
        load.start()

    barrier = pltpu.get_barrier_semaphore()

    for grp_step in range(grp_size):
        for ang_step in range(ang_size):
            if grp_step or ang_step:
                pl.semaphore_signal(
                    barrier, inc=1, device_id=(grp_at(grp_step), ang_at(ang_step)), device_id_type=MESH
                )

    loads[0].wait()
    loads[1].wait()
    sub = iota((SUBS, LANES), 0)
    octants = present.shape[1]
    mask = jnp.zeros((SUBS, LANES), F32)
    for octant in range(octants):
        mask = jnp.where(sub == octant, present[0, octant].astype(F32), mask)

    chunks = child_v.shape[0] // (2 * octants)
    chunk_tiles = child_v.shape[1] // 2
    coarse_tiles = chunks * chunk_tiles
    for row in range(child_v.shape[0]):
        slabs[row * 2 * chunk_tiles:(row + 1) * 2 * chunk_tiles, :] = child_v[row].astype(F32)
    half_width = interp.shape[0] // 2
    lane = iota((SUBS, LANES), 1)

    def shifted(here, before, by):
        return jnp.where(lane < by, pltpu.roll(before, by, 1), pltpu.roll(here, by, 1))

    for pol in range(2):
        groups = []
        for reim in range(2):
            tiles = [
                slabs[
                    pl.ds(
                        2 * chunk_tiles * (octants * chunks * reim + tile // chunk_tiles)
                        + 2 * (tile % chunk_tiles) + pol,
                        octants,
                        stride=2 * chunk_tiles * chunks,
                    ),
                    :,
                ] * mask
                for tile in range(coarse_tiles)
            ]
            groups.append(tiles)
        for tile in range(coarse_tiles):
            first = [shifted(g[tile], g[tile - 1], half_width) for g in groups]
            second = [
                shifted(g[(tile + 1) % coarse_tiles], g[tile], half_width + LANES // 2) for g in groups
            ]
            rows = slice(2 * octants * pol, 2 * octants * (pol + 1))
            lhs[tile, 0, rows, :] = jnp.concatenate(first, axis=0).astype(BF16)
            lhs[tile, 1, rows, :] = jnp.concatenate(second, axis=0).astype(BF16)

    loads[2].wait()
    loads[3].wait()
    for load in loads[4:]:
        load.start()

    band_rows = 48
    gap = iota((band_rows, LANES), 0) - iota((band_rows, LANES), 1) // 4
    band = jnp.where((gap >= 0) & (gap < SUBS), 1.0, 0.0).astype(BF16)
    turn = lane // 4

    def banded(weights):
        for step in (1, 2, 4):
            weights = jnp.where((turn & step) != 0, pltpu.roll(weights, step, 0), weights)
        high = weights.astype(BF16)
        low = (weights - high.astype(F32)).astype(BF16)
        return [jnp.concatenate([x] * (band_rows // SUBS), axis=0) * band for x in (high, low)]

    def blank(rows):
        return jnp.zeros((rows, LANES), BF16)

    def refine(block, stage):
        for half in range(2):
            x = lhs[block, half]
            cols = []
            for tile in range(2):
                at = pl.multiple_of((4 * block + 2 * half + tile) * LANES, LANES)
                pieces = []
                for piece in banded(interp[:, pl.ds(at, LANES)]):
                    pieces += [blank(32 * tile), piece] if tile else [piece]
                    pieces.append(blank(LANES - band_rows - 32 * tile))
                cols.append(jnp.concatenate(pieces, axis=0))
            stage[half] = jnp.dot(
                jnp.concatenate([x, x], axis=1), jnp.concatenate(cols, axis=1), preferred_element_type=F32
            )

    def combine(block, stage):
        real, imag = [], []
        for half in range(2):
            for tile in range(2):
                at = pl.multiple_of((4 * block + 2 * half + tile) * LANES, LANES)
                sine, cosine = sin_cos(phase[:, pl.ds(at, LANES)])
                cols = pl.ds(tile * LANES, LANES)
                for pol in range(2):
                    re = stage[half, 16 * pol:16 * pol + 8, cols]
                    im = stage[half, 16 * pol + 8:16 * pol + 16, cols]
                    real.append(re * cosine - im * sine)
                    imag.append(re * sine + im * cosine)
        send[block] = jnp.concatenate(
            [sublane_sums(real, sub), sublane_sums(imag, sub)], axis=0
        ).astype(BF16)

    def post(block, own):
        for step in range(grp_size):
            if own and not step:
                pltpu.make_async_copy(send.at[block], recv.at[me], recv_sem).start()
                continue
            pltpu.make_async_remote_copy(
                src_ref=send.at[block], dst_ref=recv.at[me], send_sem=send_sem, recv_sem=recv_sem,
                device_id=(grp_at(step), block), device_id_type=MESH,
            ).start()

    def block_at(step):
        return ang_at(1 + step)

    def refine_group(group, stages):
        for i in range(unroll):
            refine(block_at(group * unroll + i), stages.at[i])

    def combine_group(group, stages):
        for i in range(unroll):
            combine(block_at(group * unroll + i), stages.at[i])

    def post_group(group, last=False):
        for i in range(unroll):
            post(block_at(group * unroll + i), last and i == unroll - 1)

    def one_round(step, last=False):
        first = isinstance(step, int) and step == 0
        refine_group(2 * step + 1, stage_b)
        combine_group(2 * step, stage_a)
        if not first:
            post_group(2 * step)
        if not last:
            refine_group(2 * step + 2, stage_a)
        combine_group(2 * step + 1, stage_b)
        if first:
            pl.semaphore_wait(barrier, devices - 1)
            post_group(2 * step)
        post_group(2 * step + 1, last)

    def advance(step, carry):
        one_round(step)
        return carry

    refine_group(0, stage_a)
    rounds = ang_size // (2 * unroll)
    one_round(0, rounds == 1)
    if rounds > 2:
        lax.fori_loop(1, rounds - 1, advance, 0)
    if rounds > 1:
        one_round(rounds - 1, True)

    for load in loads[4:]:
        load.wait()
    slots, clusters = sources.shape
    even = (sub & 1) == 0

    def pick(cluster, carry):
        for slot in range(slots):
            both = trans[trans_ids[slot, cluster]]
            both = both * jnp.where(slot < list_len[cluster], 1.0, 0.0)
            picked[cluster * slots + slot, 0] = jnp.where(even, both, pltpu.roll(both, 1, 0))
            picked[cluster * slots + slot, 1] = jnp.where(even, pltpu.roll(both, SUBS - 1, 0), both)
        return carry

    lax.fori_loop(0, clusters, pick, 0, unroll=2)

    pltpu.make_async_copy(recv, recv, recv_sem).wait()

    def receive(cluster, carry):
        real = imag = jnp.zeros((SUBS, LANES), F32)
        for slot in range(slots):
            source = sources[slot, cluster]
            row = cluster * slots + slot
            op_re, op_im = picked[row, 0], picked[row, 1]
            both = recv[source].astype(F32)
            src_re, src_im = both[0:SUBS], both[SUBS:2 * SUBS]
            real += op_re * src_re - op_im * src_im
            imag += op_re * src_im + op_im * src_re
        for part, value in enumerate((real, imag)):
            turned[cluster, part] = value
            for pol in range(2):
                out[part, cluster, 4 * pol:4 * pol + 4, :] = turned[cluster, part, pl.ds(pol, 4, stride=2), :]
        return carry

    lax.fori_loop(0, clusters, receive, 0, unroll=4)

    sent = recv.at[pl.ds(0, devices - 1)]
    pltpu.make_async_copy(sent, sent, send_sem).wait()


def local(grp_size, ang_size, children, present, interp, phase, trans, sources, trans_ids, list_len):
    parts, own, octants, pols, angles, coarse = children.shape
    operators, width = trans.shape[1:]
    clusters, slots = sources.shape
    assert ang_size % (2 * UNROLL) == 0
    devices = grp_size * ang_size
    quarters = width // LANES
    assert (parts, own, octants, pols, angles, quarters) == (2, 1, SUBS, 2, 1, 4)
    assert interp.shape[0] == SUBS and interp.shape[1] == ang_size * width == 4 * coarse
    chunk = SUBS * LANES
    children = children.reshape(parts * octants, pols, coarse // chunk, SUBS, LANES)
    children = children.transpose(0, 2, 3, 1, 4).reshape(parts * octants * coarse // chunk, 2 * SUBS, LANES)
    trans = trans.transpose(1, 0, 2).reshape(operators, parts, quarters, LANES)
    trans = trans.transpose(0, 2, 1, 3).reshape(operators, quarters * parts, LANES)
    operands = (children, present, interp, phase, trans, sources.T, trans_ids.T, list_len)
    tile_rows = 2 * SUBS
    operands = tuple(pltpu.with_memory_space_constraint(operand, pltpu.HBM) for operand in operands)
    received = pl.pallas_call(
        functools.partial(kernel, grp_size, ang_size, UNROLL),
        out_shape=jax.ShapeDtypeStruct((parts, clusters, SUBS, LANES), F32),
        in_specs=[pl.BlockSpec(memory_space=pltpu.HBM)] * len(operands),
        out_specs=pl.BlockSpec(memory_space=pltpu.VMEM),
        scratch_shapes=[
            *(
                (pltpu.SMEM if operand.dtype == jnp.int32 else pltpu.VMEM)(operand.shape, operand.dtype)
                for operand in operands
            ),
            pltpu.VMEM((children.size // LANES, LANES), F32),
            pltpu.VMEM((coarse // LANES, 2, parts * octants * pols, LANES), BF16),
            pltpu.VMEM((UNROLL, 2, parts * octants * pols, 2 * LANES), F32),
            pltpu.VMEM((UNROLL, 2, parts * octants * pols, 2 * LANES), F32),
            pltpu.VMEM((ang_size, tile_rows, LANES), BF16),
            pltpu.VMEM((devices, tile_rows, LANES), BF16),
            pltpu.VMEM((clusters * slots, 2, SUBS, LANES), F32),
            pltpu.VMEM((clusters, 2, SUBS, LANES), F32),
            pltpu.SemaphoreType.DMA((len(operands),)),
            pltpu.SemaphoreType.DMA,
            pltpu.SemaphoreType.DMA,
        ],
        compiler_params=pltpu.CompilerParams(
            collective_id=0, has_side_effects=True, vmem_limit_bytes=48 * 1024 * 1024
        ),
    )(*operands)
    return received.reshape(parts, clusters, pols, angles, width)


def solution(mesh):
    return jax.shard_map(
        functools.partial(local, mesh.shape["grp"], mesh.shape["ang"]),
        mesh=mesh,
        in_specs=(
            P(None, ("grp", "ang"), None, None, None, None),
            P(("grp", "ang"), None),
            P(),
            P(),
            P(None, None, "ang"),
            P("grp", None),
            P("grp", None),
            P("grp"),
        ),
        out_specs=P(None, "grp", None, None, "ang"),
        check_vma=False,
    )
```
